512 devices in a mesh: blk: 8 (over z_lo), grp: 64 (over y, z_hi, x, core).
Axes of the slice: x: 4, y: 4, z: 16 (z_hi: 2, z_lo: 8; z = z_hi * 8 + z_lo), core: 2. Of those that a mesh axis runs over, the one named last changes fastest.
Arguments:
- img_feat: bfloat16 [8192, 1152], P('grp'), may hold values from -6 to 6
- txt_feat: bfloat16 [8192, 1152], P('grp'), may hold values from -6 to 6
- img_proj: bfloat16 [1152, 1152], P(None, 'grp'), may hold values from -5 to 5
- txt_proj: bfloat16 [1152, 1152], P(None, 'grp'), may hold values from -5 to 5
- logit_scale: float32 [1], replicated, may hold values from 5 to 15
- logit_bias: float32 [1], replicated, may hold values from -6 to -3
- loss_weight: float32 [1], replicated, may hold values from 15 to 60
Outputs:
- img_grad: float32 [8192, 1152], P('grp')
- txt_grad: float32 [8192, 1152], P('grp')
- img_proj_grad: float32 [1152, 1152], P(None, 'grp')
- txt_proj_grad: float32 [1152, 1152], P(None, 'grp')
The draws below stay inside these ranges and needn't reach their ends.
All inputs are finite; a program needn't handle non-finite values.
Results may differ from the reference program's by a relative error of at most 0.014.
Values may be sent and summed in bfloat16 or wider, within the bound.
No kernel may reach another device: no remote copies, remote signals or barrier semaphores. Data moves between devices by JAX's collectives and lax.ppermute only.
A program may use at most 64 MiB of HBM per device.

```python
import math
import jax
import jax.numpy as jnp
from jax import lax

W = 1152
E = 1152
BATCH = 8192
N_BLK = 8


def level_of(own_key, dims, cuts, least, largest):
    level, own = 1.0, jax.random.fold_in(own_key, 6)
    for axis_at, shards_of in cuts:
        draws = jnp.exp(jax.random.uniform(jax.random.fold_in(own, axis_at), (shards_of,), jnp.float32, least / len(cuts), largest / len(cuts)))
        level = level * jnp.repeat(draws, dims[axis_at] // shards_of).reshape([-1 if axis == axis_at else 1 for axis in range(len(dims))])
    return level


def gaussian(own_key, shape, scale, bound, shards=(), kind=jnp.bfloat16):
    drawn = scale * jax.random.normal(own_key, shape, jnp.float32)
    if shards:
        drawn = drawn * level_of(own_key, shape, shards, -0.22, 0.18)
    return jnp.clip(drawn, -bound, bound).astype(kind)


def setup_inputs(seed: int = 0) -> dict:
    seeds = jax.random.split(jax.random.key(seed), 8)
    img_feat = gaussian(seeds[0], (BATCH, W), 1.0, 6.0, ((0, 64),))
    txt_feat = gaussian(seeds[1], (BATCH, W), 1.0, 6.0, ((0, 64),))
    img_proj = gaussian(seeds[2], (W, E), 0.75, 5.0, ((1, 64),))
    txt_proj = gaussian(seeds[3], (W, E), 0.75, 5.0, ((1, 64),))
    logit_scale = jnp.clip(jnp.exp(jax.random.uniform(seeds[4], (1,), jnp.float32, math.log(5.0), math.log(15.0))), 5.0, 15.0)
    logit_bias = jnp.clip(jax.random.uniform(seeds[5], (1,), jnp.float32, -6.0, -3.0), -6.0, -3.0)
    loss_weight = jnp.clip(jnp.exp(jax.random.uniform(seeds[6], (1,), jnp.float32, math.log(15.0), math.log(60.0))), 15.0, 60.0)
    return {"img_feat": img_feat, "txt_feat": txt_feat, "img_proj": img_proj, "txt_proj": txt_proj, "logit_scale": logit_scale, "logit_bias": logit_bias, "loss_weight": loss_weight}


def embed(feat, proj):
    proj_out = jnp.dot(feat, proj, preferred_element_type=jnp.float32)
    inverse = lax.rsqrt(lax.optimization_barrier(jnp.sum(proj_out * proj_out, axis=1, keepdims=True)) + 1e-06)
    return (proj_out * inverse, inverse)

def pull_back(grad_unit, unit, inverse):
    inner = lax.optimization_barrier(jnp.sum(unit * grad_unit, axis=1, keepdims=True))
    return ((grad_unit - unit * inner) * inverse).astype(jnp.bfloat16)

def reference(img_feat, txt_feat, img_proj, txt_proj, logit_scale, logit_bias, loss_weight):
    scale = logit_scale[0]
    shift_by = logit_bias[0]
    weight = loss_weight[0]
    img_unit, img_inv = embed(img_feat, img_proj)
    txt_unit, txt_inv = embed(txt_feat, txt_proj)
    img_emb = img_unit.astype(jnp.bfloat16)
    txt_emb = txt_unit.astype(jnp.bfloat16)
    total = img_emb.shape[0]
    depth = img_emb.shape[1]
    block = total // N_BLK
    img_ids = jnp.arange(total, dtype=jnp.int32)
    blocks = txt_emb.reshape(N_BLK, block, depth)
    firsts = jnp.arange(N_BLK, dtype=jnp.int32) * block

    def visit(d_img, inputs):
        texts, first = inputs
        text_ids = first + jnp.arange(block, dtype=jnp.int32)
        logits = scale * jnp.dot(texts, img_emb.T, preferred_element_type=jnp.float32) + shift_by
        sign = jnp.where(text_ids[:, None] == img_ids[None, :], jnp.float32(1.0), jnp.float32(-1.0))
        coef = (-weight * sign * jax.nn.sigmoid(-sign * logits)).astype(jnp.bfloat16)
        d_img = d_img + jnp.dot(coef.T, texts, preferred_element_type=jnp.float32)
        d_txt = jnp.dot(coef, img_emb, preferred_element_type=jnp.float32)
        return (d_img, d_txt)
    d_img, d_txt = lax.scan(visit, jnp.zeros((total, depth), jnp.float32), (blocks, firsts))
    d_txt = d_txt.reshape(total, depth)
    img_du = pull_back(scale * d_img, img_unit, img_inv)
    txt_du = pull_back(scale * d_txt, txt_unit, txt_inv)
    img_grad = jnp.dot(img_du, img_proj.T, preferred_element_type=jnp.float32)
    txt_grad = jnp.dot(txt_du, txt_proj.T, preferred_element_type=jnp.float32)
    img_proj_grad = jnp.dot(img_feat.T, img_du, preferred_element_type=jnp.float32)
    txt_proj_grad = jnp.dot(txt_feat.T, txt_du, preferred_element_type=jnp.float32)
    return (img_grad, txt_grad, img_proj_grad, txt_proj_grad)
```

```python
import jax
import jax.numpy as jnp
from jax import lax
from jax.sharding import PartitionSpec as P

BOTH = ("blk", "grp")
N_BLK, N_Y, N_ZH, N_X, N_CORE = 8, 4, 2, 4, 2
N_GRP = N_Y * N_ZH * N_X * N_CORE
PAIR = 40


def place(blk, y, zh, x, core):
    return blk * N_GRP + ((y * N_ZH + zh) * N_X + x) * N_CORE + core


def parts(device):
    blk, grp = divmod(device, N_GRP)
    grp, core = divmod(grp, N_CORE)
    grp, x = divmod(grp, N_X)
    y, zh = divmod(grp, N_ZH)
    return blk, y, zh, x, core


def sibling(device):
    return device ^ 1


def mirror(device):
    blk, y, zh, x, core = parts(device)
    return place(N_BLK - 1 - blk, y, 1 - zh, x, core)


PLANE = [
    [place(blk, y, zh, x, core) for y in range(N_Y) for x in range(N_X)]
    for blk in range(N_BLK)
    for zh in range(N_ZH)
    for core in range(N_CORE)
]
LINE = [
    [place(sub if zh == 0 else N_BLK - 1 - sub, y, zh, x, core) for sub in range(N_BLK)]
    for y in range(N_Y)
    for zh in range(N_ZH)
    for x in range(N_X)
    for core in range(N_CORE)
]


def permuted(value, target):
    pairs = [(source, target(source)) for source in range(N_BLK * N_GRP)]
    return lax.ppermute(value, BOTH, pairs)


def exchanged(value, groups):
    return lax.all_to_all(value, BOTH, 0, 0, axis_index_groups=groups, tiled=True)


def gathered(value, groups):
    count = len(groups[0])
    copies = jnp.broadcast_to(value[None], (count,) + value.shape)
    return exchanged(copies, groups)


def contract_last(left, right):
    return lax.dot_general(
        left, right, (((1,), (1,)), ((), ())), preferred_element_type=jnp.float32
    )


def contract_first(left, right):
    return lax.dot_general(
        left, right, (((0,), (0,)), ((), ())), preferred_element_type=jnp.float32
    )


def body(img_feat, txt_feat, img_proj, txt_proj, logit_scale, logit_bias, loss_weight):
    bf16, f32 = jnp.bfloat16, jnp.float32
    scale, shift_by, weight = logit_scale[0], logit_bias[0], loss_weight[0]
    rows, width = img_feat.shape
    cols = img_proj.shape[1]
    blk = lax.axis_index("blk")
    grp = lax.axis_index("grp")
    core = grp % N_CORE
    x = (grp // N_CORE) % N_X
    zh = (grp // (N_CORE * N_X)) % N_ZH
    y = grp // (N_CORE * N_X * N_ZH)
    first = core == 0
    sub = jnp.where(zh == 0, blk, N_BLK - 1 - blk)
    sub_rows = rows // N_BLK
    own = N_CORE * rows

    img_t, txt_t = img_proj.T, txt_proj.T
    keep_t = jnp.where(first, img_t, txt_t)
    got_t = permuted(jnp.where(first, txt_t, img_t), sibling)
    block = jnp.concatenate(
        [
            jnp.where(first, keep_t, got_t),
            jnp.where(first, got_t, keep_t),
            jnp.zeros((PAIR - N_CORE * cols, width), bf16),
        ],
        0,
    )
    other = permuted(block, mirror)
    keep_f = jnp.where(first, img_feat, txt_feat)
    got_f = permuted(jnp.where(first, txt_feat, img_feat), sibling)
    feat = jnp.stack(
        [keep_f.reshape(N_BLK, sub_rows, width), got_f.reshape(N_BLK, sub_rows, width)], 1
    ).reshape(own, width)
    low = zh == 0
    block = jnp.concatenate([jnp.where(low, block, other), jnp.where(low, other, block)], 0)
    proj = gathered(block, PLANE).reshape(N_Y * N_X * N_ZH * PAIR, width)

    proj_out = contract_last(feat, proj)
    inverse = lax.rsqrt(jnp.sum(proj_out * proj_out, axis=1, keepdims=True) + 1e-06)
    unit = proj_out * inverse
    emb = unit.astype(bf16)

    mine = lax.dynamic_slice_in_dim(emb, sub * N_CORE * sub_rows, N_CORE * sub_rows, 0)
    got = permuted(mine, sibling)
    got = jnp.concatenate([got[sub_rows:], got[:sub_rows]], 0)
    others = gathered(jnp.concatenate([got, permuted(got, mirror)], 0), PLANE)
    others = others.reshape(-1, emb.shape[1])

    logits = scale * contract_last(emb, others) + shift_by
    row = lax.broadcasted_iota(jnp.int32, logits.shape, 0) - sub * (N_CORE * sub_rows)
    col = lax.broadcasted_iota(jnp.int32, logits.shape, 1) - (y * N_X + x) * (
        N_ZH * N_CORE * sub_rows
    )
    same = (row == col) & (row >= 0) & (row < N_CORE * sub_rows)
    sign = jnp.where(same, f32(1.0), f32(-1.0))
    coef = (-weight * sign * jax.nn.sigmoid(-sign * logits)).astype(bf16)
    part = jnp.dot(coef, others, preferred_element_type=f32).astype(bf16)

    pieces = exchanged(part.reshape(N_BLK, N_CORE * sub_rows, -1), LINE)
    grad_unit = scale * jnp.sum(pieces.astype(f32), 0)
    unit_sub = lax.dynamic_slice_in_dim(unit, sub * N_CORE * sub_rows, N_CORE * sub_rows, 0)
    inv_sub = lax.dynamic_slice_in_dim(inverse, sub * N_CORE * sub_rows, N_CORE * sub_rows, 0)
    inner = jnp.sum(unit_sub * grad_unit, axis=1, keepdims=True)
    du = ((grad_unit - unit_sub * inner) * inv_sub).astype(bf16)
    du = gathered(du, LINE).reshape(own, -1)

    terms = contract_first(du, feat).astype(bf16)
    terms = exchanged(terms.reshape(N_Y * N_X, N_ZH * PAIR, width), PLANE)
    terms = jnp.sum(terms.astype(f32), 0)
    lower, upper = terms[:PAIR], terms[PAIR:]
    came = permuted(jnp.where(low, upper, lower).astype(bf16), mirror)
    total = jnp.where(low, lower, upper) + came.astype(f32)
    keep_g = jnp.where(first, total[:cols], total[cols : 2 * cols])
    got_g = permuted(jnp.where(first, total[cols : 2 * cols], total[:cols]), sibling)
    img_proj_grad = jnp.where(first, keep_g, got_g).T
    txt_proj_grad = jnp.where(first, got_g, keep_g).T

    grad = jnp.dot(du, proj, preferred_element_type=f32)
    grad = grad.reshape(N_BLK, N_CORE, sub_rows, width)
    keep_r = grad[:, 0].reshape(rows, width)
    got_r = permuted(grad[:, 1].reshape(rows, width), sibling)
    img_grad = jnp.where(first, keep_r, got_r)
    txt_grad = jnp.where(first, got_r, keep_r)
    return (img_grad, txt_grad, img_proj_grad, txt_proj_grad)


def solution(mesh):
    return jax.shard_map(
        body,
        mesh=mesh,
        in_specs=(P("grp", None), P("grp", None), P(None, "grp"), P(None, "grp"), P(), P(), P()),
        out_specs=(P("grp", None), P("grp", None), P(None, "grp"), P(None, "grp")),
        check_vma=False,
    )
```

```python
import jax
import jax.numpy as jnp
from jax import lax
from jax.sharding import PartitionSpec as P

BOTH = ("blk", "grp")
N_BLK, N_Y, N_ZH, N_X, N_CORE = 8, 4, 2, 4, 2
N_GRP = N_Y * N_ZH * N_X * N_CORE


def place(blk, y, zh, x, core):
    return blk * N_GRP + ((y * N_ZH + zh) * N_X + x) * N_CORE + core


def parts(device):
    blk, grp = divmod(device, N_GRP)
    grp, core = divmod(grp, N_CORE)
    grp, x = divmod(grp, N_X)
    y, zh = divmod(grp, N_ZH)
    return blk, y, zh, x, core


def sibling(device):
    return device ^ 1


def mirror(device):
    blk, y, zh, x, core = parts(device)
    return place(N_BLK - 1 - blk, y, 1 - zh, x, core)


PLANE = [
    [place(blk, y, zh, x, core) for y in range(N_Y) for x in range(N_X)]
    for blk in range(N_BLK)
    for zh in range(N_ZH)
    for core in range(N_CORE)
]
LINE = [
    [place(sub if zh == 0 else N_BLK - 1 - sub, y, zh, x, core) for sub in range(N_BLK)]
    for y in range(N_Y)
    for zh in range(N_ZH)
    for x in range(N_X)
    for core in range(N_CORE)
]
RING = [
    LINE[(y * N_ZH * N_X + x) * N_CORE + core] + LINE[(y * N_ZH * N_X + N_X + x) * N_CORE + core]
    for y in range(N_Y)
    for x in range(N_X)
    for core in range(N_CORE)
]


def permuted(value, target):
    pairs = [(source, target(source)) for source in range(N_BLK * N_GRP)]
    return lax.ppermute(value, BOTH, pairs)


def exchanged(value, groups):
    return lax.all_to_all(value, BOTH, 0, 0, axis_index_groups=groups, tiled=True)


def gathered(value, groups):
    count = len(groups[0])
    copies = jnp.broadcast_to(value[None], (count,) + value.shape)
    return exchanged(copies, groups)


def contract_last(left, right):
    return lax.dot_general(
        left, right, (((1,), (1,)), ((), ())), preferred_element_type=jnp.float32
    )


def contract_first(left, right):
    return lax.dot_general(
        left, right, (((0,), (0,)), ((), ())), preferred_element_type=jnp.float32
    )


def body(img_feat, txt_feat, img_proj, txt_proj, logit_scale, logit_bias, loss_weight):
    bf16, f32 = jnp.bfloat16, jnp.float32
    scale, shift_by, weight = logit_scale[0], logit_bias[0], loss_weight[0]
    rows, width = img_feat.shape
    cols = img_proj.shape[1]
    blk = lax.axis_index("blk")
    grp = lax.axis_index("grp")
    core = grp % N_CORE
    x = (grp // N_CORE) % N_X
    zh = (grp // (N_CORE * N_X)) % N_ZH
    y = grp // (N_CORE * N_X * N_ZH)
    first = core == 0
    sub = jnp.where(zh == 0, blk, N_BLK - 1 - blk)
    sub_rows = rows // N_BLK
    own = N_CORE * rows

    img_t, txt_t = img_proj.T, txt_proj.T
    keep_t = jnp.where(first, img_t, txt_t)
    got_t = permuted(jnp.where(first, txt_t, img_t), sibling)
    block = jnp.concatenate(
        [jnp.where(first, keep_t, got_t), jnp.where(first, got_t, keep_t)], 0
    )
    near = gathered(block, PLANE)
    far = gathered(permuted(block, mirror), PLANE)
    keep_f = jnp.where(first, img_feat, txt_feat)
    got_f = permuted(jnp.where(first, txt_feat, img_feat), sibling)
    feat = jnp.stack(
        [keep_f.reshape(N_BLK, sub_rows, width), got_f.reshape(N_BLK, sub_rows, width)], 1
    ).reshape(own, width)
    low = zh == 0
    proj = jnp.stack([jnp.where(low, near, far), jnp.where(low, far, near)], 1)
    proj = proj.reshape(-1, width)
    embed = proj.shape[0]

    proj_out = contract_last(feat, proj)
    inverse = lax.rsqrt(jnp.sum(proj_out * proj_out, axis=1, keepdims=True) + 1e-06)
    unit = proj_out * inverse
    emb = unit.astype(bf16)

    mine = lax.dynamic_slice_in_dim(emb, sub * N_CORE * sub_rows, N_CORE * sub_rows, 0)
    far = gathered(permuted(mine, lambda device: mirror(sibling(device))), PLANE)
    got = permuted(mine, sibling)
    near = gathered(jnp.concatenate([got[sub_rows:], got[:sub_rows]], 0), PLANE)

    def weigh(others, with_own):
        logits = scale * contract_last(emb, others) + shift_by
        sign = f32(-1.0)
        if with_own:
            row = lax.broadcasted_iota(jnp.int32, logits.shape, 0) - sub * (N_CORE * sub_rows)
            col = lax.broadcasted_iota(jnp.int32, logits.shape, 1) - (y * N_X + x) * (
                N_CORE * sub_rows
            )
            same = (row == col) & (row >= 0) & (row < N_CORE * sub_rows)
            sign = jnp.where(same, f32(1.0), f32(-1.0))
        coef = (-weight * sign * jax.nn.sigmoid(-sign * logits)).astype(bf16)
        return jnp.dot(coef, others, preferred_element_type=f32)

    near, far = near.reshape(-1, embed), far.reshape(-1, embed)
    grad_unit = scale * (weigh(near, True) + weigh(far, False))
    inner = jnp.sum(unit * grad_unit, axis=1, keepdims=True)
    part = ((grad_unit - unit * inner) * inverse).astype(bf16)

    terms = contract_first(part, feat).astype(bf16)
    terms = exchanged(terms.reshape(N_Y * N_X, embed // (N_Y * N_X), width), PLANE)
    pieces = exchanged(part.reshape(N_BLK, N_CORE * sub_rows, embed), LINE)
    terms = jnp.sum(terms.astype(f32), 0).astype(bf16).reshape(N_ZH, N_CORE * cols, width)
    terms = jnp.pad(terms, ((0, 0), (0, -N_CORE * cols % N_BLK), (0, 0)))
    terms = exchanged(terms.reshape(N_ZH * N_BLK, -1, width), RING)
    terms = gathered(jnp.sum(terms.astype(f32), 0).astype(bf16), LINE)
    total = terms.reshape(-1, width).astype(f32)
    keep_g = jnp.where(first, total[:cols], total[cols : 2 * cols])
    got_g = permuted(jnp.where(first, total[cols : 2 * cols], total[:cols]), sibling)
    img_proj_grad = jnp.where(first, keep_g, got_g).T
    txt_proj_grad = jnp.where(first, got_g, keep_g).T

    du = gathered(jnp.sum(pieces.astype(f32), 0).astype(bf16), LINE).reshape(own, embed)
    grad = jnp.dot(du, proj, preferred_element_type=f32)
    grad = grad.reshape(N_BLK, N_CORE, sub_rows, width)
    keep_r = grad[:, 0].reshape(rows, width)
    got_r = permuted(grad[:, 1].reshape(rows, width), sibling)
    img_grad = jnp.where(first, keep_r, got_r)
    txt_grad = jnp.where(first, got_r, keep_r)
    return (img_grad, txt_grad, img_proj_grad, txt_proj_grad)


def solution(mesh):
    return jax.shard_map(
        body,
        mesh=mesh,
        in_specs=(P("grp", None), P("grp", None), P(None, "grp"), P(None, "grp"), P(), P(), P()),
        out_specs=(P("grp", None), P("grp", None), P(None, "grp"), P(None, "grp")),
        check_vma=False,
    )
```

```python
import jax
import jax.numpy as jnp
from jax import lax
from jax.sharding import PartitionSpec as P

BOTH = ("blk", "grp")
N_BLK, N_Y, N_ZH, N_X, N_CORE = 8, 4, 2, 4, 2
N_GRP = N_Y * N_ZH * N_X * N_CORE


def place(blk, y, zh, x, core):
    return blk * N_GRP + ((y * N_ZH + zh) * N_X + x) * N_CORE + core


def parts(device):
    blk, grp = divmod(device, N_GRP)
    grp, core = divmod(grp, N_CORE)
    grp, x = divmod(grp, N_X)
    y, zh = divmod(grp, N_ZH)
    return blk, y, zh, x, core


def sibling(device):
    return device ^ 1


def mirror(device):
    blk, y, zh, x, core = parts(device)
    return place(N_BLK - 1 - blk, y, 1 - zh, x, core)


def along(hop):
    return lambda device: device ^ (hop * N_GRP)


PLANE = [
    [place(blk, y, zh, x, core) for y in range(N_Y) for x in range(N_X)]
    for blk in range(N_BLK)
    for zh in range(N_ZH)
    for core in range(N_CORE)
]

def permuted(value, target):
    pairs = [(source, target(source)) for source in range(N_BLK * N_GRP)]
    return lax.ppermute(value, BOTH, pairs)


def exchanged(value, groups):
    return lax.all_to_all(value, BOTH, 0, 0, axis_index_groups=groups, tiled=True)


def gathered(value, groups):
    count = len(groups[0])
    copies = jnp.broadcast_to(value[None], (count,) + value.shape)
    return exchanged(copies, groups)


def contract_last(left, right):
    return lax.dot_general(
        left, right, (((1,), (1,)), ((), ())), preferred_element_type=jnp.float32
    )


def contract_first(left, right):
    return lax.dot_general(
        left, right, (((0,), (0,)), ((), ())), preferred_element_type=jnp.float32
    )


def body(img_feat, txt_feat, img_proj, txt_proj, logit_scale, logit_bias, loss_weight):
    bf16, f32 = jnp.bfloat16, jnp.float32
    scale, shift_by, weight = logit_scale[0], logit_bias[0], loss_weight[0]
    rows, width = img_feat.shape
    cols = img_proj.shape[1]
    blk = lax.axis_index("blk")
    grp = lax.axis_index("grp")
    core = grp % N_CORE
    x = (grp // N_CORE) % N_X
    zh = (grp // (N_CORE * N_X)) % N_ZH
    y = grp // (N_CORE * N_X * N_ZH)
    first = core == 0
    steps = jnp.where(zh == 0, blk, N_BLK - 1 - blk)
    sub = (steps & 1) * 4 + (steps & 2) + (steps & 4) // 4
    sub_rows = rows // N_BLK
    own = N_CORE * rows

    img_t, txt_t = img_proj.T, txt_proj.T
    keep_t = jnp.where(first, img_t, txt_t)
    got_t = permuted(jnp.where(first, txt_t, img_t), sibling)
    block = jnp.concatenate(
        [jnp.where(first, keep_t, got_t), jnp.where(first, got_t, keep_t)], 0
    )
    near = gathered(block, PLANE)
    far = gathered(permuted(block, mirror), PLANE)
    keep_f = jnp.where(first, img_feat, txt_feat)
    got_f = permuted(jnp.where(first, txt_feat, img_feat), sibling)
    feat = jnp.stack(
        [keep_f.reshape(N_BLK, sub_rows, width), got_f.reshape(N_BLK, sub_rows, width)], 1
    ).reshape(own, width)
    low = zh == 0
    proj = jnp.stack([jnp.where(low, near, far), jnp.where(low, far, near)], 1)
    proj = proj.reshape(-1, width)
    embed = proj.shape[0]

    proj_out = contract_last(feat, proj)
    inverse = lax.rsqrt(jnp.sum(proj_out * proj_out, axis=1, keepdims=True) + 1e-06)
    unit = proj_out * inverse
    emb = unit.astype(bf16)

    mine = lax.dynamic_slice_in_dim(emb, sub * N_CORE * sub_rows, N_CORE * sub_rows, 0)
    far = gathered(permuted(mine, lambda device: mirror(sibling(device))), PLANE)
    got = permuted(mine, sibling)
    near = gathered(jnp.concatenate([got[sub_rows:], got[:sub_rows]], 0), PLANE)

    def weigh(others, with_own):
        logits = scale * contract_last(emb, others) + shift_by
        sign = f32(-1.0)
        if with_own:
            row = lax.broadcasted_iota(jnp.int32, logits.shape, 0) - sub * (N_CORE * sub_rows)
            col = lax.broadcasted_iota(jnp.int32, logits.shape, 1) - (y * N_X + x) * (
                N_CORE * sub_rows
            )
            same = (row == col) & (row >= 0) & (row < N_CORE * sub_rows)
            sign = jnp.where(same, f32(1.0), f32(-1.0))
        coef = (-weight * sign * jax.nn.sigmoid(-sign * logits)).astype(bf16)
        return jnp.dot(coef, others, preferred_element_type=f32)

    near, far = near.reshape(-1, embed), far.reshape(-1, embed)
    grad_unit = scale * (weigh(near, True) + weigh(far, False))
    inner = jnp.sum(unit * grad_unit, axis=1, keepdims=True)
    part = ((grad_unit - unit * inner) * inverse).astype(bf16)

    terms = contract_first(part, feat).astype(bf16)
    terms = exchanged(terms.reshape(N_Y * N_X, embed // (N_Y * N_X), width), PLANE)
    held = part.astype(f32)
    for bit, hop in ((4, 1), (2, 2), (1, 4)):
        half = held.shape[0] // 2
        high = (sub & bit) // bit
        send = lax.dynamic_slice_in_dim(held, (1 - high) * half, half, 0).astype(bf16)
        stay = lax.dynamic_slice_in_dim(held, high * half, half, 0)
        held = stay + permuted(send, along(hop)).astype(f32)
    du = held.astype(bf16)
    for bit, hop in ((1, 4), (2, 2), (4, 1)):
        came = permuted(du, along(hop))
        high = (sub & bit) > 0
        du = jnp.concatenate([jnp.where(high, came, du), jnp.where(high, du, came)], 0)

    terms = jnp.sum(terms.astype(f32), 0)
    lower, upper = terms[: N_CORE * cols], terms[N_CORE * cols :]
    came = permuted(jnp.where(low, upper, lower).astype(bf16), mirror)
    total = jnp.where(low, lower, upper) + came.astype(f32)
    for hop in (1, 2, 4):
        sent = total.astype(bf16)
        total = sent.astype(f32) + permuted(sent, along(hop)).astype(f32)
    keep_g = jnp.where(first, total[:cols], total[cols : 2 * cols])
    got_g = permuted(jnp.where(first, total[cols : 2 * cols], total[:cols]), sibling)
    img_proj_grad = jnp.where(first, keep_g, got_g).T
    txt_proj_grad = jnp.where(first, got_g, keep_g).T

    grad = jnp.dot(du, proj, preferred_element_type=f32)
    grad = grad.reshape(N_BLK, N_CORE, sub_rows, width)
    keep_r = grad[:, 0].reshape(rows, width)
    got_r = permuted(grad[:, 1].reshape(rows, width), sibling)
    img_grad = jnp.where(first, keep_r, got_r)
    txt_grad = jnp.where(first, got_r, keep_r)
    return (img_grad, txt_grad, img_proj_grad, txt_proj_grad)


def solution(mesh):
    return jax.shard_map(
        body,
        mesh=mesh,
        in_specs=(P("grp", None), P("grp", None), P(None, "grp"), P(None, "grp"), P(), P(), P()),
        out_specs=(P("grp", None), P("grp", None), P(None, "grp"), P(None, "grp")),
        check_vma=False,
    )
```

```python
import jax
import jax.numpy as jnp
from jax import lax
from jax.sharding import PartitionSpec as P

BOTH = ("blk", "grp")
N_BLK, N_Y, N_ZH, N_X, N_CORE = 8, 4, 2, 4, 2
N_GRP = N_Y * N_ZH * N_X * N_CORE


def place(blk, y, zh, x, core):
    return blk * N_GRP + ((y * N_ZH + zh) * N_X + x) * N_CORE + core


def parts(device):
    blk, grp = divmod(device, N_GRP)
    grp, core = divmod(grp, N_CORE)
    grp, x = divmod(grp, N_X)
    y, zh = divmod(grp, N_ZH)
    return blk, y, zh, x, core


def sibling(device):
    return device ^ 1


def mirror(device):
    blk, y, zh, x, core = parts(device)
    return place(N_BLK - 1 - blk, y, 1 - zh, x, core)


def along(hop):
    return lambda device: device ^ (hop * N_GRP)


def crossed(first_axis):
    groups = []
    for blk in range(N_BLK):
        for zh in range(N_ZH):
            for core in range(N_CORE):
                along_x = (first_axis == "x") == (core == 0)
                for fixed in range(4):
                    groups.append(
                        [
                            place(blk, fixed, zh, at, core)
                            if along_x
                            else place(blk, at, zh, fixed, core)
                            for at in range(4)
                        ]
                    )
    return groups


INNER, OUTER = crossed("x"), crossed("y")


def permuted(value, target):
    pairs = [(source, target(source)) for source in range(N_BLK * N_GRP)]
    return lax.ppermute(value, BOTH, pairs)


def exchanged(value, groups):
    return lax.all_to_all(value, BOTH, 0, 0, axis_index_groups=groups, tiled=True)


def gathered(value, groups):
    count = len(groups[0])
    copies = jnp.broadcast_to(value[None], (count,) + value.shape)
    return exchanged(copies, groups)


def plane_gathered(value):
    return gathered(gathered(value, INNER), OUTER)


def summed(own, beside, across, both):
    own, beside, across, both = (v.astype(jnp.float32) for v in (own, beside, across, both))
    return (own + beside) + (across + both)


def block_transposed(value):
    side = value.shape[1] // (N_Y * N_X)
    value = value.reshape(-1, N_Y, N_X, side).transpose(0, 2, 1, 3)
    return value.reshape(-1, N_Y * N_X * side)


def contract_last(left, right):
    return lax.dot_general(
        left, right, (((1,), (1,)), ((), ())), preferred_element_type=jnp.float32
    )


def contract_first(left, right):
    return lax.dot_general(
        left, right, (((0,), (0,)), ((), ())), preferred_element_type=jnp.float32
    )


def body(img_feat, txt_feat, img_proj, txt_proj, logit_scale, logit_bias, loss_weight):
    bf16, f32 = jnp.bfloat16, jnp.float32
    scale, shift_by, weight = logit_scale[0], logit_bias[0], loss_weight[0]
    rows, width = img_feat.shape
    cols = img_proj.shape[1]
    blk = lax.axis_index("blk")
    grp = lax.axis_index("grp")
    core = grp % N_CORE
    x = (grp // N_CORE) % N_X
    zh = (grp // (N_CORE * N_X)) % N_ZH
    y = grp // (N_CORE * N_X * N_ZH)
    first = core == 0
    steps = jnp.where(zh == 0, blk, N_BLK - 1 - blk)
    sub = (steps & 1) * 4 + (steps & 2) + (steps & 4) // 4
    sub_rows = rows // N_BLK
    own = N_CORE * rows

    img_t, txt_t = img_proj.T, txt_proj.T
    keep_t = jnp.where(first, img_t, txt_t)
    got_t = permuted(jnp.where(first, txt_t, img_t), sibling)
    block = jnp.concatenate(
        [jnp.where(first, keep_t, got_t), jnp.where(first, got_t, keep_t)], 0
    )
    low = zh == 0
    other = permuted(block, mirror)
    block = jnp.concatenate([jnp.where(low, block, other), jnp.where(low, other, block)], 0)
    proj = plane_gathered(block).reshape(-1, width)
    embed = proj.shape[0]
    keep_f = jnp.where(first, img_feat, txt_feat)
    got_f = permuted(jnp.where(first, txt_feat, img_feat), sibling)
    feat = jnp.stack(
        [keep_f.reshape(N_BLK, sub_rows, width), got_f.reshape(N_BLK, sub_rows, width)], 1
    ).reshape(own, width)
    proj_out = contract_last(feat, proj)
    inverse = lax.rsqrt(jnp.sum(proj_out * proj_out, axis=1, keepdims=True) + 1e-06)
    unit = proj_out * inverse
    emb = unit.astype(bf16)

    mine = lax.dynamic_slice_in_dim(emb, sub * N_CORE * sub_rows, N_CORE * sub_rows, 0)
    far = permuted(mine, lambda device: mirror(sibling(device)))
    got = permuted(mine, sibling)
    near = jnp.concatenate([got[sub_rows:], got[:sub_rows]], 0)
    near = plane_gathered(block_transposed(near)).reshape(-1, embed)
    far = plane_gathered(block_transposed(far)).reshape(-1, embed)
    spot = jnp.where(first, y * N_X + x, x * N_Y + y) * (N_CORE * sub_rows)

    def weigh(others, with_own):
        logits = scale * contract_last(emb, others) + shift_by
        sign = f32(-1.0)
        if with_own:
            row = lax.broadcasted_iota(jnp.int32, logits.shape, 0) - sub * (N_CORE * sub_rows)
            col = lax.broadcasted_iota(jnp.int32, logits.shape, 1) - spot
            same = (row == col) & (row >= 0) & (row < N_CORE * sub_rows)
            sign = jnp.where(same, f32(1.0), f32(-1.0))
        coef = (-weight * sign * jax.nn.sigmoid(-sign * logits)).astype(bf16)
        return jnp.dot(coef, others, preferred_element_type=f32)

    grad_unit = scale * (weigh(near, True) + weigh(far, False))
    inner = jnp.sum(unit * grad_unit, axis=1, keepdims=True)
    part = ((grad_unit - unit * inner) * inverse).astype(bf16)

    terms = contract_first(part, feat).astype(bf16)
    part, terms = lax.optimization_barrier((part, terms))
    terms = exchanged(terms.reshape(N_Y, embed // N_Y, width), OUTER)
    terms = jnp.sum(terms.astype(f32), 0).astype(bf16)
    terms = exchanged(terms.reshape(N_X, embed // (N_Y * N_X), width), INNER)
    held = part.astype(f32)
    for bit, hop in ((4, 1), (2, 2), (1, 4)):
        half = held.shape[0] // 2
        high = (sub & bit) // bit
        send = lax.dynamic_slice_in_dim(held, (1 - high) * half, half, 0).astype(bf16)
        stay = lax.dynamic_slice_in_dim(held, high * half, half, 0)
        held = stay + permuted(send, along(hop)).astype(f32)
    du = held.astype(bf16)
    for bit, hop in ((1, 4), (2, 2), (4, 1)):
        came = permuted(du, along(hop))
        high = (sub & bit) > 0
        du = jnp.concatenate([jnp.where(high, came, du), jnp.where(high, du, came)], 0)

    terms = jnp.sum(terms.astype(f32), 0).astype(bf16)
    lower, upper = terms[: N_CORE * cols], terms[N_CORE * cols :]
    stay, send = jnp.where(low, lower, upper), jnp.where(low, upper, lower)
    total = summed(
        stay,
        permuted(stay, along(4)),
        permuted(send, mirror),
        permuted(send, lambda device: mirror(along(4)(device))),
    ).astype(bf16)
    total = summed(total, *(permuted(total, along(hop)) for hop in (1, 2, 3)))
    keep_g = jnp.where(first, total[:cols], total[cols : 2 * cols])
    got_g = permuted(jnp.where(first, total[cols : 2 * cols], total[:cols]), sibling)
    img_proj_grad = jnp.where(first, keep_g, got_g).T
    txt_proj_grad = jnp.where(first, got_g, keep_g).T

    grad = jnp.dot(du, proj, preferred_element_type=f32)
    grad = grad.reshape(N_BLK, N_CORE, sub_rows, width)
    keep_r = grad[:, 0].reshape(rows, width)
    got_r = permuted(grad[:, 1].reshape(rows, width), sibling)
    img_grad = jnp.where(first, keep_r, got_r)
    txt_grad = jnp.where(first, got_r, keep_r)
    return (img_grad, txt_grad, img_proj_grad, txt_proj_grad)


def solution(mesh):
    return jax.shard_map(
        body,
        mesh=mesh,
        in_specs=(P("grp", None), P("grp", None), P(None, "grp"), P(None, "grp"), P(), P(), P()),
        out_specs=(P("grp", None), P("grp", None), P(None, "grp"), P(None, "grp")),
        check_vma=False,
    )
```

```python
import jax
import jax.numpy as jnp
from jax import lax
from jax.sharding import PartitionSpec as P

BOTH = ("blk", "grp")
N_BLK, N_Y, N_ZH, N_X, N_CORE = 8, 4, 2, 4, 2
N_GRP = N_Y * N_ZH * N_X * N_CORE


def place(blk, y, zh, x, core):
    return blk * N_GRP + ((y * N_ZH + zh) * N_X + x) * N_CORE + core


def parts(device):
    blk, grp = divmod(device, N_GRP)
    grp, core = divmod(grp, N_CORE)
    grp, x = divmod(grp, N_X)
    y, zh = divmod(grp, N_ZH)
    return blk, y, zh, x, core


def sibling(device):
    return device ^ 1


def mirror(device):
    blk, y, zh, x, core = parts(device)
    return place(N_BLK - 1 - blk, y, 1 - zh, x, core)


def along(hop):
    return lambda device: device ^ (hop * N_GRP)


def crossed(first_axis):
    groups = []
    for blk in range(N_BLK):
        for zh in range(N_ZH):
            for core in range(N_CORE):
                along_x = (first_axis == "x") == (core == 0)
                for fixed in range(4):
                    groups.append(
                        [
                            place(blk, fixed, zh, at, core)
                            if along_x
                            else place(blk, at, zh, fixed, core)
                            for at in range(4)
                        ]
                    )
    return groups


INNER, OUTER = crossed("x"), crossed("y")
PLANE = [
    [
        place(blk, slow, zh, fast, core) if core == 0 else place(blk, fast, zh, slow, core)
        for slow in range(4)
        for fast in range(4)
    ]
    for blk in range(N_BLK)
    for zh in range(N_ZH)
    for core in range(N_CORE)
]
LINE = [[place(blk, *rest) for blk in range(N_BLK)] for rest in map(lambda d: parts(d)[1:], range(N_GRP))]


def permuted(value, target):
    pairs = [(source, target(source)) for source in range(N_BLK * N_GRP)]
    return lax.ppermute(value, BOTH, pairs)


def exchanged(value, groups):
    return lax.all_to_all(value, BOTH, 0, 0, axis_index_groups=groups, tiled=True)


def gathered(value, groups):
    count = len(groups[0])
    copies = jnp.broadcast_to(value[None], (count,) + value.shape)
    return exchanged(copies, groups)


def contract_last(left, right):
    return lax.dot_general(
        left, right, (((1,), (1,)), ((), ())), preferred_element_type=jnp.float32
    )


def contract_first(left, right):
    return lax.dot_general(
        left, right, (((0,), (0,)), ((), ())), preferred_element_type=jnp.float32
    )


def body(img_feat, txt_feat, img_proj, txt_proj, logit_scale, logit_bias, loss_weight):
    bf16, f32 = jnp.bfloat16, jnp.float32
    scale, shift_by, weight = logit_scale[0], logit_bias[0], loss_weight[0]
    rows, width = img_feat.shape
    cols = img_proj.shape[1]
    blk = lax.axis_index("blk")
    grp = lax.axis_index("grp")
    core = grp % N_CORE
    x = (grp // N_CORE) % N_X
    zh = (grp // (N_CORE * N_X)) % N_ZH
    y = grp // (N_CORE * N_X * N_ZH)
    first = core == 0
    steps = jnp.where(zh == 0, blk, N_BLK - 1 - blk)
    sub = (steps & 1) * 4 + (steps & 2) + (steps & 4) // 4
    sub_rows = rows // N_BLK
    own = N_CORE * rows

    low = zh == 0
    img_t, txt_t = img_proj.T, txt_proj.T
    keep_t = jnp.where(first, img_t, txt_t)
    keep_f = jnp.where(first, img_feat, txt_feat)
    give_f = jnp.where(first, txt_feat, img_feat)
    give_sub = lax.dynamic_slice_in_dim(keep_f, sub * sub_rows, sub_rows, 0)
    keep_sub = lax.dynamic_slice_in_dim(give_f, sub * sub_rows, sub_rows, 0)
    got = permuted(jnp.concatenate([jnp.where(first, txt_t, img_t), give_sub], 0), sibling)
    got_t, got_sub = got[:cols], got[cols:]
    pair = N_CORE * cols
    near = jnp.concatenate(
        [jnp.where(first, keep_t, got_t), jnp.where(first, got_t, keep_t), keep_sub, got_sub], 0
    )
    far = gathered(permuted(near, mirror), INNER)
    near = gathered(near, INNER)
    proj = jnp.concatenate(
        [
            jnp.where(low, near[:, :pair], far[:, :pair]),
            jnp.where(low, far[:, :pair], near[:, :pair]),
        ],
        1,
    )
    others = jnp.concatenate([near[:, pair:], far[:, pair:]], 1)
    proj, others = lax.optimization_barrier((gathered(proj, OUTER), others))
    others = gathered(others, OUTER).reshape(-1, width)
    other_proj = permuted(proj, sibling).transpose(1, 0, 2, 3).reshape(-1, width)
    proj = proj.reshape(-1, width)
    embed = proj.shape[0]

    got_f = permuted(give_f, sibling)
    feat = jnp.stack(
        [keep_f.reshape(N_BLK, sub_rows, width), got_f.reshape(N_BLK, sub_rows, width)], 1
    ).reshape(own, width)

    def embedded(rows_of, columns_of):
        proj_out = contract_last(rows_of, columns_of)
        inverse = lax.rsqrt(jnp.sum(proj_out * proj_out, axis=1, keepdims=True) + 1e-06)
        return proj_out * inverse, inverse

    unit, inverse = embedded(feat, proj)
    emb = unit.astype(bf16)
    others = embedded(others, other_proj)[0].astype(bf16)
    spot = jnp.where(first, y * N_X + x, x * N_Y + y) * (N_ZH * N_CORE * sub_rows)

    logits = scale * contract_last(emb, others) + shift_by
    row = lax.broadcasted_iota(jnp.int32, logits.shape, 0) - sub * (N_CORE * sub_rows)
    col = lax.broadcasted_iota(jnp.int32, logits.shape, 1) - spot
    same = (row == col) & (row >= 0) & (row < N_CORE * sub_rows)
    sign = jnp.where(same, f32(1.0), f32(-1.0))
    coef = (-weight * sign * jax.nn.sigmoid(-sign * logits)).astype(bf16)
    grad_unit = scale * jnp.dot(coef, others, preferred_element_type=f32)
    inner = jnp.sum(unit * grad_unit, axis=1, keepdims=True)
    part = ((grad_unit - unit * inner) * inverse).astype(bf16)

    terms = contract_first(part, feat).astype(bf16)
    part, terms = lax.optimization_barrier((part, terms))
    terms = exchanged(terms.reshape(N_Y * N_X, embed // (N_Y * N_X), width), PLANE)
    held = part.astype(f32)
    for bit, hop in ((4, 1), (2, 2), (1, 4)):
        half = held.shape[0] // 2
        high = (sub & bit) // bit
        send = lax.dynamic_slice_in_dim(held, (1 - high) * half, half, 0).astype(bf16)
        stay = lax.dynamic_slice_in_dim(held, high * half, half, 0)
        held = stay + permuted(send, along(hop)).astype(f32)
    du, terms = lax.optimization_barrier((held.astype(bf16), terms))
    for bit, hop in ((1, 4), (2, 2), (4, 1)):
        came = permuted(du, along(hop))
        high = (sub & bit) > 0
        du = jnp.concatenate([jnp.where(high, came, du), jnp.where(high, du, came)], 0)

    terms = jnp.sum(terms.astype(f32), 0)
    lower, upper = terms[:pair], terms[pair:]
    came = permuted(jnp.where(low, upper, lower).astype(bf16), mirror)
    terms = (jnp.where(low, lower, upper) + came.astype(f32)).astype(bf16)
    terms = jnp.pad(terms, ((0, -pair % N_BLK), (0, 0))).reshape(N_BLK, -1, width)
    terms = jnp.sum(exchanged(terms, LINE).astype(f32), 0).astype(bf16)
    total = gathered(terms, LINE).reshape(-1, width).astype(f32)
    keep_g = jnp.where(first, total[:cols], total[cols : 2 * cols])
    got_g = permuted(jnp.where(first, total[cols : 2 * cols], total[:cols]), sibling)
    img_proj_grad = jnp.where(first, keep_g, got_g).T
    txt_proj_grad = jnp.where(first, got_g, keep_g).T

    grad = jnp.dot(du, proj, preferred_element_type=f32)
    grad = grad.reshape(N_BLK, N_CORE, sub_rows, width)
    keep_r = grad[:, 0].reshape(rows, width)
    got_r = permuted(grad[:, 1].reshape(rows, width), sibling)
    img_grad = jnp.where(first, keep_r, got_r)
    txt_grad = jnp.where(first, got_r, keep_r)
    return (img_grad, txt_grad, img_proj_grad, txt_proj_grad)


def solution(mesh):
    return jax.shard_map(
        body,
        mesh=mesh,
        in_specs=(P("grp", None), P("grp", None), P(None, "grp"), P(None, "grp"), P(), P(), P()),
        out_specs=(P("grp", None), P("grp", None), P(None, "grp"), P(None, "grp")),
        check_vma=False,
    )
```

```python
import jax
import jax.numpy as jnp
from jax import lax
from jax.sharding import PartitionSpec as P

BOTH = ("blk", "grp")
N_BLK, N_Y, N_ZH, N_X, N_CORE = 8, 4, 2, 4, 2
N_GRP = N_Y * N_ZH * N_X * N_CORE


def place(blk, y, zh, x, core):
    return blk * N_GRP + ((y * N_ZH + zh) * N_X + x) * N_CORE + core


def parts(device):
    blk, grp = divmod(device, N_GRP)
    grp, core = divmod(grp, N_CORE)
    grp, x = divmod(grp, N_X)
    y, zh = divmod(grp, N_ZH)
    return blk, y, zh, x, core


def sibling(device):
    return device ^ 1


def mirror(device):
    blk, y, zh, x, core = parts(device)
    return place(N_BLK - 1 - blk, y, 1 - zh, x, core)


def along(hop):
    return lambda device: device ^ (hop * N_GRP)


def crossed(first_axis):
    groups = []
    for blk in range(N_BLK):
        for zh in range(N_ZH):
            for core in range(N_CORE):
                along_x = (first_axis == "x") == (core == 0)
                for fixed in range(4):
                    groups.append(
                        [
                            place(blk, fixed, zh, at, core)
                            if along_x
                            else place(blk, at, zh, fixed, core)
                            for at in range(4)
                        ]
                    )
    return groups


INNER, OUTER = crossed("x"), crossed("y")
PLANE = [
    [place(blk, y, zh, x, core) for y in range(N_Y) for x in range(N_X)]
    for blk in range(N_BLK)
    for zh in range(N_ZH)
    for core in range(N_CORE)
]
LINE = [[place(blk, *rest) for blk in range(N_BLK)] for rest in map(lambda d: parts(d)[1:], range(N_GRP))]


def permuted(value, target):
    pairs = [(source, target(source)) for source in range(N_BLK * N_GRP)]
    return lax.ppermute(value, BOTH, pairs)


def exchanged(value, groups):
    return lax.all_to_all(value, BOTH, 0, 0, axis_index_groups=groups, tiled=True)


def gathered(value, groups):
    count = len(groups[0])
    copies = jnp.broadcast_to(value[None], (count,) + value.shape)
    return exchanged(copies, groups)


def contract_last(left, right):
    return lax.dot_general(
        left, right, (((1,), (1,)), ((), ())), preferred_element_type=jnp.float32
    )


def contract_first(left, right):
    return lax.dot_general(
        left, right, (((0,), (0,)), ((), ())), preferred_element_type=jnp.float32
    )


def body(img_feat, txt_feat, img_proj, txt_proj, logit_scale, logit_bias, loss_weight):
    bf16, f32 = jnp.bfloat16, jnp.float32
    scale, shift_by, weight = logit_scale[0], logit_bias[0], loss_weight[0]
    rows, width = img_feat.shape
    cols = img_proj.shape[1]
    blk = lax.axis_index("blk")
    grp = lax.axis_index("grp")
    core = grp % N_CORE
    x = (grp // N_CORE) % N_X
    zh = (grp // (N_CORE * N_X)) % N_ZH
    y = grp // (N_CORE * N_X * N_ZH)
    first = core == 0
    steps = jnp.where(zh == 0, blk, N_BLK - 1 - blk)
    sub = (steps & 1) * 4 + (steps & 2) + (steps & 4) // 4
    sub_rows = rows // N_BLK
    own = N_CORE * rows

    low = zh == 0
    img_t, txt_t = img_proj.T, txt_proj.T
    own_f, other_f = jnp.where(first, img_feat, txt_feat), jnp.where(first, txt_feat, img_feat)
    own_sub = lax.dynamic_slice_in_dim(own_f, sub * sub_rows, sub_rows, 0)
    other_sub = lax.dynamic_slice_in_dim(other_f, sub * sub_rows, sub_rows, 0)
    ours = jnp.concatenate([own_sub, jnp.where(first, img_t, txt_t)], 0)
    theirs = jnp.concatenate([other_sub, jnp.where(first, txt_t, img_t)], 0)

    def joined(mine, siblings):
        mine_t, siblings_t = mine[sub_rows:], siblings[sub_rows:]
        return jnp.concatenate(
            [
                mine[:sub_rows],
                siblings[:sub_rows],
                jnp.where(first, mine_t, siblings_t),
                jnp.where(first, siblings_t, mine_t),
            ],
            0,
        )

    far = joined(
        permuted(ours, mirror), permuted(theirs, lambda device: mirror(sibling(device)))
    )
    near = gathered(joined(ours, permuted(theirs, sibling)), INNER)
    far = gathered(far, INNER)
    picked = N_CORE * sub_rows
    pair = N_CORE * cols
    both = jnp.concatenate(
        [
            near[:, :picked],
            far[:, :picked],
            jnp.where(low, near[:, picked:], far[:, picked:]),
            jnp.where(low, far[:, picked:], near[:, picked:]),
        ],
        1,
    )
    both = gathered(both, OUTER)
    others = both[:, :, : N_ZH * picked].reshape(-1, width)
    proj = both[:, :, N_ZH * picked :]
    proj = jnp.where(first, proj, proj.transpose(1, 0, 2, 3)).reshape(-1, width)
    embed = proj.shape[0]

    sib_feat = permuted(jnp.concatenate([own_f, other_f], 0), sibling)
    sib_other, sib_own = sib_feat[:rows], sib_feat[rows:]

    def interleaved(one, two):
        shape = (N_BLK, sub_rows, width)
        return jnp.stack([one.reshape(shape), two.reshape(shape)], 1).reshape(own, width)

    feat = interleaved(other_f, sib_other)

    def normalized(proj_out):
        inverse = lax.rsqrt(jnp.sum(proj_out * proj_out, axis=1, keepdims=True) + 1e-06)
        return proj_out * inverse, inverse

    made = contract_last(interleaved(sib_own, own_f), proj)
    unit, inverse = normalized(permuted(made, sibling))
    emb = unit.astype(bf16)
    others = normalized(contract_last(others, proj))[0].astype(bf16)
    spot = jnp.where(first, y * N_X + x, x * N_Y + y) * (N_ZH * picked)

    logits = scale * contract_last(emb, others) + shift_by
    row = lax.broadcasted_iota(jnp.int32, logits.shape, 0) - sub * (N_CORE * sub_rows)
    col = lax.broadcasted_iota(jnp.int32, logits.shape, 1) - spot
    same = (row == col) & (row >= 0) & (row < N_CORE * sub_rows)
    sign = jnp.where(same, f32(1.0), f32(-1.0))
    coef = (-weight * sign * jax.nn.sigmoid(-sign * logits)).astype(bf16)
    grad_unit = scale * jnp.dot(coef, others, preferred_element_type=f32)
    inner = jnp.sum(unit * grad_unit, axis=1, keepdims=True)
    part = ((grad_unit - unit * inner) * inverse).astype(bf16)

    terms = contract_first(part, feat).astype(bf16)
    part, terms = lax.optimization_barrier((part, terms))
    terms = exchanged(terms.reshape(N_Y * N_X, embed // (N_Y * N_X), width), PLANE)
    held = part.astype(f32)
    for bit, hop in ((4, 1), (2, 2), (1, 4)):
        half = held.shape[0] // 2
        high = (sub & bit) // bit
        send = lax.dynamic_slice_in_dim(held, (1 - high) * half, half, 0).astype(bf16)
        stay = lax.dynamic_slice_in_dim(held, high * half, half, 0)
        held = stay + permuted(send, along(hop)).astype(f32)
    du, terms = lax.optimization_barrier((held.astype(bf16), terms))
    for bit, hop in ((1, 4), (2, 2), (4, 1)):
        came = permuted(du, along(hop))
        high = (sub & bit) > 0
        du = jnp.concatenate([jnp.where(high, came, du), jnp.where(high, du, came)], 0)

    terms = jnp.sum(terms.astype(f32), 0)
    lower, upper = terms[:pair], terms[pair:]
    came = permuted(jnp.where(low, upper, lower).astype(bf16), mirror)
    terms = (jnp.where(low, lower, upper) + came.astype(f32)).astype(bf16)
    terms = jnp.pad(terms, ((0, -pair % N_BLK), (0, 0))).reshape(N_BLK, -1, width)
    terms = jnp.sum(exchanged(terms, LINE).astype(f32), 0).astype(bf16)
    total = gathered(terms, LINE).reshape(-1, width).astype(f32)
    keep_g = jnp.where(first, total[:cols], total[cols:pair])
    got_g = permuted(jnp.where(first, total[cols:pair], total[:cols]), sibling)
    img_proj_grad = jnp.where(first, got_g, keep_g).T
    txt_proj_grad = jnp.where(first, keep_g, got_g).T

    grad = jnp.dot(du, permuted(proj, sibling), preferred_element_type=f32)
    grad = grad.reshape(N_BLK, N_CORE, sub_rows, width)
    keep_r = grad[:, 0].reshape(rows, width)
    got_r = permuted(grad[:, 1].reshape(rows, width), sibling)
    img_grad = jnp.where(first, got_r, keep_r)
    txt_grad = jnp.where(first, keep_r, got_r)
    return (img_grad, txt_grad, img_proj_grad, txt_proj_grad)


def solution(mesh):
    return jax.shard_map(
        body,
        mesh=mesh,
        in_specs=(P("grp", None), P("grp", None), P(None, "grp"), P(None, "grp"), P(), P(), P()),
        out_specs=(P("grp", None), P("grp", None), P(None, "grp"), P(None, "grp")),
        check_vma=False,
    )
```

```python
import jax
import jax.numpy as jnp
from jax import lax
from jax.sharding import PartitionSpec as P

BOTH = ("blk", "grp")
N_BLK, N_Y, N_ZH, N_X, N_CORE = 8, 4, 2, 4, 2
N_GRP = N_Y * N_ZH * N_X * N_CORE


def place(blk, y, zh, x, core):
    return blk * N_GRP + ((y * N_ZH + zh) * N_X + x) * N_CORE + core


def parts(device):
    blk, grp = divmod(device, N_GRP)
    grp, core = divmod(grp, N_CORE)
    grp, x = divmod(grp, N_X)
    y, zh = divmod(grp, N_ZH)
    return blk, y, zh, x, core


def sibling(device):
    return device ^ 1


def mirror(device):
    blk, y, zh, x, core = parts(device)
    return place(N_BLK - 1 - blk, y, 1 - zh, x, core)


def along(hop):
    return lambda device: device ^ (hop * N_GRP)


def crossed(first_axis):
    groups = []
    for blk in range(N_BLK):
        for zh in range(N_ZH):
            for core in range(N_CORE):
                along_x = (first_axis == "x") == (core == 0)
                for fixed in range(4):
                    groups.append(
                        [
                            place(blk, fixed, zh, at, core)
                            if along_x
                            else place(blk, at, zh, fixed, core)
                            for at in range(4)
                        ]
                    )
    return groups


INNER, OUTER = crossed("x"), crossed("y")
PLANE = [
    [place(blk, y, zh, x, core) for y in range(N_Y) for x in range(N_X)]
    for blk in range(N_BLK)
    for zh in range(N_ZH)
    for core in range(N_CORE)
]


def permuted(value, target):
    pairs = [(source, target(source)) for source in range(N_BLK * N_GRP)]
    return lax.ppermute(value, BOTH, pairs)


def exchanged(value, groups):
    return lax.all_to_all(value, BOTH, 0, 0, axis_index_groups=groups, tiled=True)


def gathered(value, groups):
    count = len(groups[0])
    copies = jnp.broadcast_to(value[None], (count,) + value.shape)
    return exchanged(copies, groups)


def contract_last(left, right):
    return lax.dot_general(
        left, right, (((1,), (1,)), ((), ())), preferred_element_type=jnp.float32
    )


def contract_first(left, right):
    return lax.dot_general(
        left, right, (((0,), (0,)), ((), ())), preferred_element_type=jnp.float32
    )


def body(img_feat, txt_feat, img_proj, txt_proj, logit_scale, logit_bias, loss_weight):
    bf16, f32 = jnp.bfloat16, jnp.float32
    scale, shift_by, weight = logit_scale[0], logit_bias[0], loss_weight[0]
    rows, width = img_feat.shape
    cols = img_proj.shape[1]
    blk = lax.axis_index("blk")
    grp = lax.axis_index("grp")
    core = grp % N_CORE
    x = (grp // N_CORE) % N_X
    zh = (grp // (N_CORE * N_X)) % N_ZH
    y = grp // (N_CORE * N_X * N_ZH)
    first = core == 0
    steps = jnp.where(zh == 0, blk, N_BLK - 1 - blk)
    sub = (steps & 1) * 4 + (steps & 2) + (steps & 4) // 4
    sub_rows = rows // N_BLK
    own = N_CORE * rows

    low = zh == 0
    img_t, txt_t = img_proj.T, txt_proj.T
    own_f, other_f = jnp.where(first, img_feat, txt_feat), jnp.where(first, txt_feat, img_feat)
    own_sub = lax.dynamic_slice_in_dim(own_f, sub * sub_rows, sub_rows, 0)
    other_sub = lax.dynamic_slice_in_dim(other_f, sub * sub_rows, sub_rows, 0)
    ours = jnp.concatenate([own_sub, jnp.where(first, img_t, txt_t)], 0)
    theirs = jnp.concatenate([other_sub, jnp.where(first, txt_t, img_t)], 0)

    def joined(mine, siblings):
        mine_t, siblings_t = mine[sub_rows:], siblings[sub_rows:]
        return jnp.concatenate(
            [
                mine[:sub_rows],
                siblings[:sub_rows],
                jnp.where(first, mine_t, siblings_t),
                jnp.where(first, siblings_t, mine_t),
            ],
            0,
        )

    far = joined(
        permuted(ours, mirror), permuted(theirs, lambda device: mirror(sibling(device)))
    )
    near = gathered(joined(ours, permuted(theirs, sibling)), INNER)
    far = gathered(far, INNER)
    picked = N_CORE * sub_rows
    pair = N_CORE * cols
    both = jnp.concatenate(
        [
            near[:, :picked],
            far[:, :picked],
            jnp.where(low, near[:, picked:], far[:, picked:]),
            jnp.where(low, far[:, picked:], near[:, picked:]),
        ],
        1,
    )
    both = gathered(both, OUTER)
    others = both[:, :, : N_ZH * picked].reshape(-1, width)
    proj = both[:, :, N_ZH * picked :]
    proj = jnp.where(first, proj, proj.transpose(1, 0, 2, 3)).reshape(-1, width)
    embed = proj.shape[0]

    sib_feat = permuted(jnp.concatenate([own_f, other_f], 0), sibling)
    sib_other, sib_own = sib_feat[:rows], sib_feat[rows:]

    def interleaved(one, two):
        shape = (N_BLK, sub_rows, width)
        return jnp.stack([one.reshape(shape), two.reshape(shape)], 1).reshape(own, width)

    feat = interleaved(other_f, sib_other)

    def normalized(proj_out):
        inverse = lax.rsqrt(jnp.sum(proj_out * proj_out, axis=1, keepdims=True) + 1e-06)
        return proj_out * inverse, inverse

    made = contract_last(interleaved(sib_own, own_f), proj)
    unit, inverse = normalized(permuted(made, sibling))
    emb = unit.astype(bf16)
    others = normalized(contract_last(others, proj))[0].astype(bf16)
    spot = jnp.where(first, y * N_X + x, x * N_Y + y) * (N_ZH * picked)

    logits = scale * contract_last(emb, others) + shift_by
    row = lax.broadcasted_iota(jnp.int32, logits.shape, 0) - sub * (N_CORE * sub_rows)
    col = lax.broadcasted_iota(jnp.int32, logits.shape, 1) - spot
    same = (row == col) & (row >= 0) & (row < N_CORE * sub_rows)
    sign = jnp.where(same, f32(1.0), f32(-1.0))
    coef = (-weight * sign * jax.nn.sigmoid(-sign * logits)).astype(bf16)
    grad_unit = scale * jnp.dot(coef, others, preferred_element_type=f32)
    inner = jnp.sum(unit * grad_unit, axis=1, keepdims=True)
    part = ((grad_unit - unit * inner) * inverse).astype(bf16)

    part = part.astype(f32) + permuted(part, along(1)).astype(f32)
    odd = (steps & 1) == 1
    half = width // 2
    terms = contract_first(part.astype(bf16), jnp.where(odd, feat[:, half:], feat[:, :half]))
    part, terms = lax.optimization_barrier((part, terms.astype(bf16)))
    terms = exchanged(terms.reshape(N_Y * N_X, embed // (N_Y * N_X), half), PLANE)
    held = lax.dynamic_slice_in_dim(part, (steps & 1) * (own // 2), own // 2, 0)
    for bit, hop in ((2, 2), (1, 4)):
        count = held.shape[0] // 2
        high = (sub & bit) // bit
        send = lax.dynamic_slice_in_dim(held, (1 - high) * count, count, 0).astype(bf16)
        stay = lax.dynamic_slice_in_dim(held, high * count, count, 0)
        held = stay + permuted(send, along(hop)).astype(f32)
    du, terms = lax.optimization_barrier((held.astype(bf16), terms))
    for bit, hop in ((1, 4), (2, 2), (4, 1)):
        came = permuted(du, along(hop))
        high = (sub & bit) > 0
        du = jnp.concatenate([jnp.where(high, came, du), jnp.where(high, du, came)], 0)

    terms = jnp.sum(terms.astype(f32), 0)
    lower, upper = terms[:pair], terms[pair:]
    came = permuted(jnp.where(low, upper, lower).astype(bf16), mirror)
    total = jnp.where(low, lower, upper) + came.astype(f32)
    for hop in (2, 4):
        total = total.astype(bf16)
        total = total.astype(f32) + permuted(total, along(hop)).astype(f32)
    came = permuted(total, along(1))
    total = jnp.concatenate([jnp.where(odd, came, total), jnp.where(odd, total, came)], 1)
    keep_g = jnp.where(first, total[:cols], total[cols:pair])
    got_g = permuted(jnp.where(first, total[cols:pair], total[:cols]), sibling)
    img_proj_grad = jnp.where(first, got_g, keep_g).T
    txt_proj_grad = jnp.where(first, keep_g, got_g).T

    grad = jnp.dot(du, permuted(proj, sibling), preferred_element_type=f32)
    grad = grad.reshape(N_BLK, N_CORE, sub_rows, width)
    keep_r = grad[:, 0].reshape(rows, width)
    got_r = permuted(grad[:, 1].reshape(rows, width), sibling)
    img_grad = jnp.where(first, got_r, keep_r)
    txt_grad = jnp.where(first, keep_r, got_r)
    return (img_grad, txt_grad, img_proj_grad, txt_proj_grad)


def solution(mesh):
    return jax.shard_map(
        body,
        mesh=mesh,
        in_specs=(P("grp", None), P("grp", None), P(None, "grp"), P(None, "grp"), P(), P(), P()),
        out_specs=(P("grp", None), P("grp", None), P(None, "grp"), P(None, "grp")),
        check_vma=False,
    )
```

```python
import functools

import jax
import jax.numpy as jnp
from jax import lax
from jax.experimental import pallas as pl
from jax.experimental.pallas import tpu as pltpu
from jax.sharding import PartitionSpec as P

BOTH = ("blk", "grp")
N_BLK, N_Y, N_ZH, N_X, N_CORE = 8, 4, 2, 4, 2
N_GRP = N_Y * N_ZH * N_X * N_CORE


def place(blk, y, zh, x, core):
    return blk * N_GRP + ((y * N_ZH + zh) * N_X + x) * N_CORE + core


def parts(device):
    blk, grp = divmod(device, N_GRP)
    grp, core = divmod(grp, N_CORE)
    grp, x = divmod(grp, N_X)
    y, zh = divmod(grp, N_ZH)
    return blk, y, zh, x, core


def sibling(device):
    return device ^ 1


def mirror(device):
    blk, y, zh, x, core = parts(device)
    return place(N_BLK - 1 - blk, y, 1 - zh, x, core)


def along(hop):
    return lambda device: device ^ (hop * N_GRP)


def crossed(first_axis):
    groups = []
    for blk in range(N_BLK):
        for zh in range(N_ZH):
            for core in range(N_CORE):
                along_x = (first_axis == "x") == (core == 0)
                for fixed in range(4):
                    groups.append(
                        [
                            place(blk, fixed, zh, at, core)
                            if along_x
                            else place(blk, at, zh, fixed, core)
                            for at in range(4)
                        ]
                    )
    return groups


INNER, OUTER = crossed("x"), crossed("y")
PLANE = [
    [place(blk, y, zh, x, core) for y in range(N_Y) for x in range(N_X)]
    for blk in range(N_BLK)
    for zh in range(N_ZH)
    for core in range(N_CORE)
]

RING = [
    [
        place(step if zh == 0 else N_BLK - 1 - step, y, zh, x, core)
        for zh in range(N_ZH)
        for step in range(odd, N_BLK, 2)
    ]
    for odd in range(2)
    for y in range(N_Y)
    for x in range(N_X)
    for core in range(N_CORE)
]


def permuted(value, target):
    pairs = [(source, target(source)) for source in range(N_BLK * N_GRP)]
    return lax.ppermute(value, BOTH, pairs)


def exchanged(value, groups):
    return lax.all_to_all(value, BOTH, 0, 0, axis_index_groups=groups, tiled=True)


def gathered(value, groups):
    count = len(groups[0])
    copies = jnp.broadcast_to(value[None], (count,) + value.shape)
    return exchanged(copies, groups)


def contract_last(left, right):
    return lax.dot_general(
        left, right, (((1,), (1,)), ((), ())), preferred_element_type=jnp.float32
    )


def contract_first(left, right):
    return lax.dot_general(
        left, right, (((0,), (0,)), ((), ())), preferred_element_type=jnp.float32
    )


def embed_kernel(feat_ref, proj_ref, emb_ref):
    proj_out = contract_last(feat_ref[...].reshape(emb_ref.shape), proj_ref[...])
    inverse = lax.rsqrt(jnp.sum(proj_out * proj_out, axis=1, keepdims=True) + 1e-06)
    emb_ref[...] = (proj_out * inverse).astype(jnp.bfloat16)


def embedded(both, picked, proj):
    count, _, width = both.shape
    embed = proj.shape[0]
    group = 4
    rows = count * picked
    return pl.pallas_call(
        embed_kernel,
        grid=(count // group,),
        in_specs=[
            pl.BlockSpec((group, picked, width), lambda i: (i, 0, 0)),
            pl.BlockSpec((embed, width), lambda i: (0, 0)),
        ],
        out_specs=pl.BlockSpec((group * picked, embed), lambda i: (i, 0)),
        out_shape=jax.ShapeDtypeStruct((rows, embed), jnp.bfloat16),
        compiler_params=pltpu.CompilerParams(vmem_limit_bytes=40 * 2**20),
        cost_estimate=pl.CostEstimate(
            flops=2 * rows * embed * width,
            bytes_accessed=2 * (rows * width + rows * embed + embed * width),
            transcendentals=rows,
        ),
    )(both, proj)


def partial_kernel(at_ref, par_ref, made_ref, others_ref, part_ref, emb_ref, acc_ref, *, block):
    step = pl.program_id(0)
    scale, shift_by, weight = par_ref[0], par_ref[1], par_ref[2]

    def unit_of():
        made = made_ref[...]
        inverse = lax.rsqrt(jnp.sum(made * made, axis=1, keepdims=True) + 1e-06)
        return made * inverse, inverse

    @pl.when(step == 0)
    def _():
        emb_ref[...] = unit_of()[0].astype(jnp.bfloat16)
        acc_ref[...] = jnp.zeros_like(acc_ref)

    others = others_ref[...]
    logits = scale * contract_last(emb_ref[...], others) + shift_by
    row = lax.broadcasted_iota(jnp.int32, logits.shape, 0) - at_ref[0]
    col = lax.broadcasted_iota(jnp.int32, logits.shape, 1) + (step * logits.shape[1] - at_ref[1])
    same = (row == col) & (row >= 0) & (row < block)
    coef = jnp.where(same, -weight, weight) * jax.nn.sigmoid(jnp.where(same, -logits, logits))
    acc_ref[...] += jnp.dot(
        coef.astype(jnp.bfloat16), others, preferred_element_type=jnp.float32
    )

    @pl.when(step == pl.num_programs(0) - 1)
    def _():
        unit, inverse = unit_of()
        grad_unit = scale * acc_ref[...]
        inner = jnp.sum(unit * grad_unit, axis=1, keepdims=True)
        part_ref[...] = ((grad_unit - unit * inner) * inverse).astype(jnp.bfloat16)


def partial_grads(at, params, made, others, block):
    own, embed = made.shape
    count = others.shape[0]
    tile = 256
    return pl.pallas_call(
        functools.partial(partial_kernel, block=block),
        grid=(count // tile,),
        in_specs=[
            pl.BlockSpec(memory_space=pltpu.SMEM),
            pl.BlockSpec(memory_space=pltpu.SMEM),
            pl.BlockSpec((own, embed), lambda i: (0, 0)),
            pl.BlockSpec((tile, embed), lambda i: (i, 0)),
        ],
        out_specs=pl.BlockSpec((own, embed), lambda i: (0, 0)),
        out_shape=jax.ShapeDtypeStruct((own, embed), jnp.bfloat16),
        scratch_shapes=[
            pltpu.VMEM((own, embed), jnp.bfloat16),
            pltpu.VMEM((own, embed), jnp.float32),
        ],
        compiler_params=pltpu.CompilerParams(vmem_limit_bytes=40 * 2**20),
        cost_estimate=pl.CostEstimate(
            flops=4 * own * count * embed,
            bytes_accessed=2 * count * embed + 6 * own * embed,
            transcendentals=own * count,
        ),
    )(at, params, made, others)


def body(img_feat, txt_feat, img_proj, txt_proj, logit_scale, logit_bias, loss_weight):
    bf16, f32 = jnp.bfloat16, jnp.float32
    scale, shift_by, weight = logit_scale[0], logit_bias[0], loss_weight[0]
    rows, width = img_feat.shape
    cols = img_proj.shape[1]
    blk = lax.axis_index("blk")
    grp = lax.axis_index("grp")
    core = grp % N_CORE
    x = (grp // N_CORE) % N_X
    zh = (grp // (N_CORE * N_X)) % N_ZH
    y = grp // (N_CORE * N_X * N_ZH)
    first = core == 0
    steps = jnp.where(zh == 0, blk, N_BLK - 1 - blk)
    sub = (steps & 1) * 4 + (steps & 2) + (steps & 4) // 4
    sub_rows = rows // N_BLK
    own = N_CORE * rows

    low = zh == 0
    img_t, txt_t = img_proj.T, txt_proj.T
    own_f, other_f = jnp.where(first, img_feat, txt_feat), jnp.where(first, txt_feat, img_feat)
    own_sub = lax.dynamic_slice_in_dim(own_f, sub * sub_rows, sub_rows, 0)
    other_sub = lax.dynamic_slice_in_dim(other_f, sub * sub_rows, sub_rows, 0)
    ours = jnp.concatenate([own_sub, jnp.where(first, img_t, txt_t)], 0)
    theirs = jnp.concatenate([other_sub, jnp.where(first, txt_t, img_t)], 0)

    def joined(mine, siblings):
        mine_t, siblings_t = mine[sub_rows:], siblings[sub_rows:]
        return jnp.concatenate(
            [
                mine[:sub_rows],
                siblings[:sub_rows],
                jnp.where(first, mine_t, siblings_t),
                jnp.where(first, siblings_t, mine_t),
            ],
            0,
        )

    far = joined(
        permuted(ours, mirror), permuted(theirs, lambda device: mirror(sibling(device)))
    )
    near = gathered(joined(ours, permuted(theirs, sibling)), INNER)
    far = gathered(far, INNER)
    picked = N_CORE * sub_rows
    pair = N_CORE * cols
    both = jnp.concatenate(
        [
            near[:, :picked],
            far[:, :picked],
            jnp.where(low, near[:, picked:], far[:, picked:]),
            jnp.where(low, far[:, picked:], near[:, picked:]),
        ],
        1,
    )
    both = gathered(both, OUTER)
    proj = both[:, :, N_ZH * picked :]
    proj = jnp.where(first, proj, proj.transpose(1, 0, 2, 3)).reshape(-1, width)
    embed = proj.shape[0]

    sib_feat = permuted(jnp.concatenate([own_f, other_f], 0), sibling)
    sib_other, sib_own = sib_feat[:rows], sib_feat[rows:]

    def interleaved(one, two):
        shape = (N_BLK, sub_rows, width)
        return jnp.stack([one.reshape(shape), two.reshape(shape)], 1).reshape(own, width)

    feat = interleaved(other_f, sib_other)

    made = permuted(contract_last(interleaved(sib_own, own_f), proj), sibling)
    others = embedded(both.reshape(N_Y * N_X, -1, width), N_ZH * picked, proj)
    spot = jnp.where(first, y * N_X + x, x * N_Y + y) * (N_ZH * picked)
    at = jnp.stack([sub * picked, spot]).astype(jnp.int32)
    part = partial_grads(at, jnp.stack([scale, shift_by, weight]), made, others, picked)
    part, other_proj = lax.optimization_barrier((part, permuted(proj, sibling)))

    part = part.astype(f32) + permuted(part, along(1)).astype(f32)
    odd = (steps & 1) == 1
    half = width // 2
    terms = contract_first(part.astype(bf16), jnp.where(odd, feat[:, half:], feat[:, :half]))
    part, terms = lax.optimization_barrier((part, terms.astype(bf16)))
    terms = exchanged(terms.reshape(N_Y * N_X, embed // (N_Y * N_X), half), PLANE)
    held = lax.dynamic_slice_in_dim(part, (steps & 1) * (own // 2), own // 2, 0)
    for bit, hop in ((2, 2), (1, 4)):
        count = held.shape[0] // 2
        high = (sub & bit) // bit
        send = lax.dynamic_slice_in_dim(held, (1 - high) * count, count, 0).astype(bf16)
        stay = lax.dynamic_slice_in_dim(held, high * count, count, 0)
        held = stay + permuted(send, along(hop)).astype(f32)
    du, terms = lax.optimization_barrier((held.astype(bf16), terms))
    for bit, hop in ((1, 4), (2, 2), (4, 1)):
        came = permuted(du, along(hop))
        high = (sub & bit) > 0
        du = jnp.concatenate([jnp.where(high, came, du), jnp.where(high, du, came)], 0)

    terms = jnp.sum(terms.astype(f32), 0)
    terms = terms.astype(bf16).reshape(N_ZH, pair, half)
    terms = jnp.broadcast_to(terms[:, None], (N_ZH, N_BLK // 2, pair, half))
    terms = exchanged(terms.reshape(N_BLK, pair, half), RING)
    total = jnp.sum(terms.astype(f32), 0)
    came = permuted(total, along(1))
    total = jnp.concatenate([jnp.where(odd, came, total), jnp.where(odd, total, came)], 1)
    keep_g = jnp.where(first, total[:cols], total[cols:pair])
    got_g = permuted(jnp.where(first, total[cols:pair], total[:cols]), sibling)
    img_proj_grad = jnp.where(first, got_g, keep_g).T
    txt_proj_grad = jnp.where(first, keep_g, got_g).T

    grad = jnp.dot(du, other_proj, preferred_element_type=f32)
    grad = grad.reshape(N_BLK, N_CORE, sub_rows, width)
    keep_r = grad[:, 0].reshape(rows, width)
    got_r = permuted(grad[:, 1].reshape(rows, width), sibling)
    img_grad = jnp.where(first, got_r, keep_r)
    txt_grad = jnp.where(first, keep_r, got_r)
    return (img_grad, txt_grad, img_proj_grad, txt_proj_grad)


def solution(mesh):
    return jax.shard_map(
        body,
        mesh=mesh,
        in_specs=(P("grp", None), P("grp", None), P(None, "grp"), P(None, "grp"), P(), P(), P()),
        out_specs=(P("grp", None), P("grp", None), P(None, "grp"), P(None, "grp")),
        check_vma=False,
    )
```

```python
import functools

import jax
import jax.numpy as jnp
from jax import lax
from jax.experimental import pallas as pl
from jax.experimental.pallas import tpu as pltpu
from jax.sharding import PartitionSpec as P

BOTH = ("blk", "grp")
N_BLK, N_Y, N_ZH, N_X, N_CORE = 8, 4, 2, 4, 2
N_GRP = N_Y * N_ZH * N_X * N_CORE


def place(blk, y, zh, x, core):
    return blk * N_GRP + ((y * N_ZH + zh) * N_X + x) * N_CORE + core


def parts(device):
    blk, grp = divmod(device, N_GRP)
    grp, core = divmod(grp, N_CORE)
    grp, x = divmod(grp, N_X)
    y, zh = divmod(grp, N_ZH)
    return blk, y, zh, x, core


def sibling(device):
    return device ^ 1


def mirror(device):
    blk, y, zh, x, core = parts(device)
    return place(N_BLK - 1 - blk, y, 1 - zh, x, core)


def along(hop):
    return lambda device: device ^ (hop * N_GRP)


def crossed(first_axis):
    groups = []
    for blk in range(N_BLK):
        for zh in range(N_ZH):
            for core in range(N_CORE):
                along_x = (first_axis == "x") == (core == 0)
                for fixed in range(4):
                    groups.append(
                        [
                            place(blk, fixed, zh, at, core)
                            if along_x
                            else place(blk, at, zh, fixed, core)
                            for at in range(4)
                        ]
                    )
    return groups


INNER, OUTER = crossed("x"), crossed("y")
PLANE = [
    [place(blk, y, zh, x, core) for y in range(N_Y) for x in range(N_X)]
    for blk in range(N_BLK)
    for zh in range(N_ZH)
    for core in range(N_CORE)
]

RING = [
    [
        place(step if zh == 0 else N_BLK - 1 - step, y, zh, x, core)
        for zh in range(N_ZH)
        for step in range(odd, N_BLK, 2)
    ]
    for odd in range(2)
    for y in range(N_Y)
    for x in range(N_X)
    for core in range(N_CORE)
]


def permuted(value, target):
    pairs = [(source, target(source)) for source in range(N_BLK * N_GRP)]
    return lax.ppermute(value, BOTH, pairs)


def exchanged(value, groups):
    return lax.all_to_all(value, BOTH, 0, 0, axis_index_groups=groups, tiled=True)


def gathered(value, groups):
    count = len(groups[0])
    copies = jnp.broadcast_to(value[None], (count,) + value.shape)
    return exchanged(copies, groups)


def contract_last(left, right):
    return lax.dot_general(
        left, right, (((1,), (1,)), ((), ())), preferred_element_type=jnp.float32
    )


def contract_first(left, right):
    return lax.dot_general(
        left, right, (((0,), (0,)), ((), ())), preferred_element_type=jnp.float32
    )


def embed_kernel(feat_ref, proj_ref, emb_ref):
    proj_out = contract_last(feat_ref[...].reshape(emb_ref.shape), proj_ref[...])
    inverse = lax.rsqrt(jnp.sum(proj_out * proj_out, axis=1, keepdims=True) + 1e-06)
    emb_ref[...] = (proj_out * inverse).astype(jnp.bfloat16)


def embedded(both, picked, proj):
    count, _, width = both.shape
    embed = proj.shape[0]
    group = 8
    rows = count * picked
    return pl.pallas_call(
        embed_kernel,
        grid=(count // group,),
        in_specs=[
            pl.BlockSpec((group, picked, width), lambda i: (i, 0, 0)),
            pl.BlockSpec((embed, width), lambda i: (0, 0)),
        ],
        out_specs=pl.BlockSpec((group * picked, embed), lambda i: (i, 0)),
        out_shape=jax.ShapeDtypeStruct((rows, embed), jnp.bfloat16),
        compiler_params=pltpu.CompilerParams(vmem_limit_bytes=40 * 2**20),
        cost_estimate=pl.CostEstimate(
            flops=2 * rows * embed * width,
            bytes_accessed=2 * (rows * width + rows * embed + embed * width),
            transcendentals=rows,
        ),
    )(both, proj)


def partial_kernel(at_ref, par_ref, made_ref, others_ref, part_ref, emb_ref, acc_ref, *, block):
    step = pl.program_id(0)
    scale, shift_by, weight = par_ref[0], par_ref[1], par_ref[2]

    def unit_of():
        made = made_ref[...]
        inverse = lax.rsqrt(jnp.sum(made * made, axis=1, keepdims=True) + 1e-06)
        return made * inverse, inverse

    @pl.when(step == 0)
    def _():
        emb_ref[...] = unit_of()[0].astype(jnp.bfloat16)
        acc_ref[...] = jnp.zeros_like(acc_ref)

    others = others_ref[...]
    logits = scale * contract_last(emb_ref[...], others) + shift_by
    row = lax.broadcasted_iota(jnp.int32, logits.shape, 0) - at_ref[0]
    col = lax.broadcasted_iota(jnp.int32, logits.shape, 1) + (step * logits.shape[1] - at_ref[1])
    same = (row == col) & (row >= 0) & (row < block)
    coef = jnp.where(same, -weight, weight) * jax.nn.sigmoid(jnp.where(same, -logits, logits))
    acc_ref[...] += jnp.dot(
        coef.astype(jnp.bfloat16), others, preferred_element_type=jnp.float32
    )

    @pl.when(step == pl.num_programs(0) - 1)
    def _():
        unit, inverse = unit_of()
        grad_unit = scale * acc_ref[...]
        inner = jnp.sum(unit * grad_unit, axis=1, keepdims=True)
        part_ref[...] = ((grad_unit - unit * inner) * inverse).astype(jnp.bfloat16)


def partial_grads(at, params, made, others, block):
    own, embed = made.shape
    count = others.shape[0]
    tile = count
    return pl.pallas_call(
        functools.partial(partial_kernel, block=block),
        grid=(count // tile,),
        in_specs=[
            pl.BlockSpec(memory_space=pltpu.SMEM),
            pl.BlockSpec(memory_space=pltpu.SMEM),
            pl.BlockSpec((own, embed), lambda i: (0, 0)),
            pl.BlockSpec((tile, embed), lambda i: (i, 0)),
        ],
        out_specs=pl.BlockSpec((own, embed), lambda i: (0, 0)),
        out_shape=jax.ShapeDtypeStruct((own, embed), jnp.bfloat16),
        scratch_shapes=[
            pltpu.VMEM((own, embed), jnp.bfloat16),
            pltpu.VMEM((own, embed), jnp.float32),
        ],
        compiler_params=pltpu.CompilerParams(vmem_limit_bytes=40 * 2**20),
        cost_estimate=pl.CostEstimate(
            flops=4 * own * count * embed,
            bytes_accessed=2 * count * embed + 6 * own * embed,
            transcendentals=own * count,
        ),
    )(at, params, made, others)


def body(img_feat, txt_feat, img_proj, txt_proj, logit_scale, logit_bias, loss_weight):
    bf16, f32 = jnp.bfloat16, jnp.float32
    scale, shift_by, weight = logit_scale[0], logit_bias[0], loss_weight[0]
    rows, width = img_feat.shape
    cols = img_proj.shape[1]
    blk = lax.axis_index("blk")
    grp = lax.axis_index("grp")
    core = grp % N_CORE
    x = (grp // N_CORE) % N_X
    zh = (grp // (N_CORE * N_X)) % N_ZH
    y = grp // (N_CORE * N_X * N_ZH)
    first = core == 0
    steps = jnp.where(zh == 0, blk, N_BLK - 1 - blk)
    sub = (steps & 1) * 4 + (steps & 2) + (steps & 4) // 4
    sub_rows = rows // N_BLK
    own = N_CORE * rows

    low = zh == 0
    img_t, txt_t = img_proj.T, txt_proj.T
    own_f, other_f = jnp.where(first, img_feat, txt_feat), jnp.where(first, txt_feat, img_feat)
    own_sub = lax.dynamic_slice_in_dim(own_f, sub * sub_rows, sub_rows, 0)
    other_sub = lax.dynamic_slice_in_dim(other_f, sub * sub_rows, sub_rows, 0)
    ours = jnp.concatenate([own_sub, jnp.where(first, img_t, txt_t)], 0)
    theirs = jnp.concatenate([other_sub, jnp.where(first, txt_t, img_t)], 0)

    def joined(mine, siblings):
        mine_t, siblings_t = mine[sub_rows:], siblings[sub_rows:]
        return jnp.concatenate(
            [
                mine[:sub_rows],
                siblings[:sub_rows],
                jnp.where(first, mine_t, siblings_t),
                jnp.where(first, siblings_t, mine_t),
            ],
            0,
        )

    far = joined(
        permuted(ours, mirror), permuted(theirs, lambda device: mirror(sibling(device)))
    )
    near = gathered(joined(ours, permuted(theirs, sibling)), INNER)
    far = gathered(far, INNER)
    picked = N_CORE * sub_rows
    pair = N_CORE * cols
    both = jnp.concatenate(
        [
            near[:, :picked],
            far[:, :picked],
            jnp.where(low, near[:, picked:], far[:, picked:]),
            jnp.where(low, far[:, picked:], near[:, picked:]),
        ],
        1,
    )
    sib_feat = permuted(jnp.concatenate([own_f, other_f], 0), sibling)
    sib_other, sib_own = sib_feat[:rows], sib_feat[rows:]

    def interleaved(one, two):
        shape = (N_BLK, sub_rows, width)
        return jnp.stack([one.reshape(shape), two.reshape(shape)], 1).reshape(own, width)

    feat = interleaved(other_f, sib_other)
    sib_rows = interleaved(sib_own, own_f)
    both, feat, sib_rows = lax.optimization_barrier((both, feat, sib_rows))

    both = gathered(both, OUTER)
    proj = both[:, :, N_ZH * picked :]
    proj = jnp.where(first, proj, proj.transpose(1, 0, 2, 3)).reshape(-1, width)
    embed = proj.shape[0]

    made = permuted(contract_last(sib_rows, proj), sibling)
    others = embedded(both.reshape(N_Y * N_X, -1, width), N_ZH * picked, proj)
    spot = jnp.where(first, y * N_X + x, x * N_Y + y) * (N_ZH * picked)
    at = jnp.stack([sub * picked, spot]).astype(jnp.int32)
    part = partial_grads(at, jnp.stack([scale, shift_by, weight]), made, others, picked)

    part = part.astype(f32) + permuted(part, along(1)).astype(f32)
    odd = (steps & 1) == 1
    half = width // 2
    terms = contract_first(part.astype(bf16), jnp.where(odd, feat[:, half:], feat[:, :half]))
    part, terms = lax.optimization_barrier((part, terms.astype(bf16)))
    terms = exchanged(terms.reshape(N_Y * N_X, embed // (N_Y * N_X), half), PLANE)
    held = lax.dynamic_slice_in_dim(part, (steps & 1) * (own // 2), own // 2, 0)
    for bit, hop in ((2, 2), (1, 4)):
        count = held.shape[0] // 2
        high = (sub & bit) // bit
        send = lax.dynamic_slice_in_dim(held, (1 - high) * count, count, 0).astype(bf16)
        stay = lax.dynamic_slice_in_dim(held, high * count, count, 0)
        held = stay + permuted(send, along(hop)).astype(f32)
    du, terms, other_proj = lax.optimization_barrier(
        (held.astype(bf16), terms, permuted(proj, sibling))
    )
    terms = jnp.sum(terms.astype(f32), 0).astype(bf16).reshape(N_ZH, pair, half)
    terms = jnp.broadcast_to(terms[:, None], (N_ZH, N_BLK // 2, pair, half))
    terms = exchanged(terms.reshape(N_BLK, pair, half), RING)
    for bit, hop in ((1, 4), (2, 2), (4, 1)):
        if hop == 1:
            du, terms = lax.optimization_barrier((du, terms))
        came = permuted(du, along(hop))
        high = (sub & bit) > 0
        du = jnp.concatenate([jnp.where(high, came, du), jnp.where(high, du, came)], 0)
    total = jnp.sum(terms.astype(f32), 0)
    came = permuted(total, along(1))
    total = jnp.concatenate([jnp.where(odd, came, total), jnp.where(odd, total, came)], 1)
    keep_g = jnp.where(first, total[:cols], total[cols:pair])
    got_g = permuted(jnp.where(first, total[cols:pair], total[:cols]), sibling)
    img_proj_grad = jnp.where(first, got_g, keep_g).T
    txt_proj_grad = jnp.where(first, keep_g, got_g).T

    du = du.reshape(N_BLK, N_CORE, sub_rows, embed)

    def grads(core_at):
        rows_of = du[:, core_at].reshape(rows, embed)
        return jnp.dot(rows_of, other_proj, preferred_element_type=f32)

    got_r = permuted(grads(1), sibling)
    keep_r = grads(0)
    img_grad = jnp.where(first, got_r, keep_r)
    txt_grad = jnp.where(first, keep_r, got_r)
    return (img_grad, txt_grad, img_proj_grad, txt_proj_grad)


def solution(mesh):
    return jax.shard_map(
        body,
        mesh=mesh,
        in_specs=(P("grp", None), P("grp", None), P(None, "grp"), P(None, "grp"), P(), P(), P()),
        out_specs=(P("grp", None), P("grp", None), P(None, "grp"), P(None, "grp")),
        check_vma=False,
    )
```

```python
import functools

import jax
import jax.numpy as jnp
from jax import lax
from jax.experimental import pallas as pl
from jax.experimental.pallas import tpu as pltpu
from jax.sharding import PartitionSpec as P

BOTH = ("blk", "grp")
N_BLK, N_Y, N_ZH, N_X, N_CORE = 8, 4, 2, 4, 2
N_GRP = N_Y * N_ZH * N_X * N_CORE


def place(blk, y, zh, x, core):
    return blk * N_GRP + ((y * N_ZH + zh) * N_X + x) * N_CORE + core


def parts(device):
    blk, grp = divmod(device, N_GRP)
    grp, core = divmod(grp, N_CORE)
    grp, x = divmod(grp, N_X)
    y, zh = divmod(grp, N_ZH)
    return blk, y, zh, x, core


def sibling(device):
    return device ^ 1


def mirror(device):
    blk, y, zh, x, core = parts(device)
    return place(N_BLK - 1 - blk, y, 1 - zh, x, core)


def along(hop):
    return lambda device: device ^ (hop * N_GRP)


def crossed(first_axis):
    groups = []
    for blk in range(N_BLK):
        for zh in range(N_ZH):
            for core in range(N_CORE):
                along_x = (first_axis == "x") == (core == 0)
                for fixed in range(4):
                    groups.append(
                        [
                            place(blk, fixed, zh, at, core)
                            if along_x
                            else place(blk, at, zh, fixed, core)
                            for at in range(4)
                        ]
                    )
    return groups


INNER, OUTER = crossed("x"), crossed("y")
PLANE = [
    [place(blk, y, zh, x, core) for y in range(N_Y) for x in range(N_X)]
    for blk in range(N_BLK)
    for zh in range(N_ZH)
    for core in range(N_CORE)
]


def permuted(value, target):
    pairs = [(source, target(source)) for source in range(N_BLK * N_GRP)]
    return lax.ppermute(value, BOTH, pairs)


def exchanged(value, groups):
    return lax.all_to_all(value, BOTH, 0, 0, axis_index_groups=groups, tiled=True)


def gathered(value, groups):
    count = len(groups[0])
    copies = jnp.broadcast_to(value[None], (count,) + value.shape)
    return exchanged(copies, groups)


def summed(own, beside, across, both):
    own, beside, across, both = (v.astype(jnp.float32) for v in (own, beside, across, both))
    return (own + beside) + (across + both)


def contract_last(left, right):
    return lax.dot_general(
        left, right, (((1,), (1,)), ((), ())), preferred_element_type=jnp.float32
    )


def contract_first(left, right):
    return lax.dot_general(
        left, right, (((0,), (0,)), ((), ())), preferred_element_type=jnp.float32
    )


def embed_kernel(feat_ref, proj_ref, emb_ref):
    proj_out = contract_last(feat_ref[...].reshape(emb_ref.shape), proj_ref[...])
    inverse = lax.rsqrt(jnp.sum(proj_out * proj_out, axis=1, keepdims=True) + 1e-06)
    emb_ref[...] = (proj_out * inverse).astype(jnp.bfloat16)


def embedded(both, picked, proj):
    count, _, width = both.shape
    embed = proj.shape[0]
    group = 8
    rows = count * picked
    return pl.pallas_call(
        embed_kernel,
        grid=(count // group,),
        in_specs=[
            pl.BlockSpec((group, picked, width), lambda i: (i, 0, 0)),
            pl.BlockSpec((embed, width), lambda i: (0, 0)),
        ],
        out_specs=pl.BlockSpec((group * picked, embed), lambda i: (i, 0)),
        out_shape=jax.ShapeDtypeStruct((rows, embed), jnp.bfloat16),
        compiler_params=pltpu.CompilerParams(vmem_limit_bytes=40 * 2**20),
        cost_estimate=pl.CostEstimate(
            flops=2 * rows * embed * width,
            bytes_accessed=2 * (rows * width + rows * embed + embed * width),
            transcendentals=rows,
        ),
    )(both, proj)


def partial_kernel(at_ref, par_ref, made_ref, others_ref, part_ref, emb_ref, acc_ref, *, block):
    step = pl.program_id(0)
    scale, shift_by, weight = par_ref[0], par_ref[1], par_ref[2]

    def unit_of():
        made = made_ref[...]
        inverse = lax.rsqrt(jnp.sum(made * made, axis=1, keepdims=True) + 1e-06)
        return made * inverse, inverse

    @pl.when(step == 0)
    def _():
        emb_ref[...] = unit_of()[0].astype(jnp.bfloat16)
        acc_ref[...] = jnp.zeros_like(acc_ref)

    others = others_ref[...]
    logits = scale * contract_last(emb_ref[...], others) + shift_by
    row = lax.broadcasted_iota(jnp.int32, logits.shape, 0) - at_ref[0]
    col = lax.broadcasted_iota(jnp.int32, logits.shape, 1) + (step * logits.shape[1] - at_ref[1])
    same = (row == col) & (row >= 0) & (row < block)
    coef = jnp.where(same, -weight, weight) * jax.nn.sigmoid(jnp.where(same, -logits, logits))
    acc_ref[...] += jnp.dot(
        coef.astype(jnp.bfloat16), others, preferred_element_type=jnp.float32
    )

    @pl.when(step == pl.num_programs(0) - 1)
    def _():
        unit, inverse = unit_of()
        grad_unit = scale * acc_ref[...]
        inner = jnp.sum(unit * grad_unit, axis=1, keepdims=True)
        part_ref[...] = ((grad_unit - unit * inner) * inverse).astype(jnp.bfloat16)


def partial_grads(at, params, made, others, block):
    own, embed = made.shape
    count = others.shape[0]
    tile = count
    return pl.pallas_call(
        functools.partial(partial_kernel, block=block),
        grid=(count // tile,),
        in_specs=[
            pl.BlockSpec(memory_space=pltpu.SMEM),
            pl.BlockSpec(memory_space=pltpu.SMEM),
            pl.BlockSpec((own, embed), lambda i: (0, 0)),
            pl.BlockSpec((tile, embed), lambda i: (i, 0)),
        ],
        out_specs=pl.BlockSpec((own, embed), lambda i: (0, 0)),
        out_shape=jax.ShapeDtypeStruct((own, embed), jnp.bfloat16),
        scratch_shapes=[
            pltpu.VMEM((own, embed), jnp.bfloat16),
            pltpu.VMEM((own, embed), jnp.float32),
        ],
        compiler_params=pltpu.CompilerParams(vmem_limit_bytes=40 * 2**20),
        cost_estimate=pl.CostEstimate(
            flops=4 * own * count * embed,
            bytes_accessed=2 * count * embed + 6 * own * embed,
            transcendentals=own * count,
        ),
    )(at, params, made, others)


def body(img_feat, txt_feat, img_proj, txt_proj, logit_scale, logit_bias, loss_weight):
    bf16, f32 = jnp.bfloat16, jnp.float32
    scale, shift_by, weight = logit_scale[0], logit_bias[0], loss_weight[0]
    rows, width = img_feat.shape
    cols = img_proj.shape[1]
    blk = lax.axis_index("blk")
    grp = lax.axis_index("grp")
    core = grp % N_CORE
    x = (grp // N_CORE) % N_X
    zh = (grp // (N_CORE * N_X)) % N_ZH
    y = grp // (N_CORE * N_X * N_ZH)
    first = core == 0
    steps = jnp.where(zh == 0, blk, N_BLK - 1 - blk)
    sub = (steps & 1) * 4 + (steps & 2) + (steps & 4) // 4
    sub_rows = rows // N_BLK
    own = N_CORE * rows

    low = zh == 0
    img_t, txt_t = img_proj.T, txt_proj.T
    own_f, other_f = jnp.where(first, img_feat, txt_feat), jnp.where(first, txt_feat, img_feat)
    own_sub = lax.dynamic_slice_in_dim(own_f, sub * sub_rows, sub_rows, 0)
    other_sub = lax.dynamic_slice_in_dim(other_f, sub * sub_rows, sub_rows, 0)
    ours = jnp.concatenate([own_sub, jnp.where(first, img_t, txt_t)], 0)
    theirs = jnp.concatenate([other_sub, jnp.where(first, txt_t, img_t)], 0)

    def joined(mine, siblings):
        mine_t, siblings_t = mine[sub_rows:], siblings[sub_rows:]
        return jnp.concatenate(
            [
                mine[:sub_rows],
                siblings[:sub_rows],
                jnp.where(first, mine_t, siblings_t),
                jnp.where(first, siblings_t, mine_t),
            ],
            0,
        )

    far = joined(
        permuted(ours, mirror), permuted(theirs, lambda device: mirror(sibling(device)))
    )
    near = gathered(joined(ours, permuted(theirs, sibling)), INNER)
    far = gathered(far, INNER)
    picked = N_CORE * sub_rows
    pair = N_CORE * cols
    both = jnp.concatenate(
        [
            near[:, :picked],
            far[:, :picked],
            jnp.where(low, near[:, picked:], far[:, picked:]),
            jnp.where(low, far[:, picked:], near[:, picked:]),
        ],
        1,
    )
    sib_feat = permuted(jnp.concatenate([own_f, other_f], 0), sibling)
    sib_other, sib_own = sib_feat[:rows], sib_feat[rows:]

    def interleaved(one, two):
        shape = (N_BLK, sub_rows, width)
        return jnp.stack([one.reshape(shape), two.reshape(shape)], 1).reshape(own, width)

    feat = interleaved(other_f, sib_other)
    sib_rows = interleaved(sib_own, own_f)
    both, feat, sib_rows = lax.optimization_barrier((both, feat, sib_rows))

    both = gathered(both, OUTER)
    proj = both[:, :, N_ZH * picked :]
    proj = jnp.where(first, proj, proj.transpose(1, 0, 2, 3)).reshape(-1, width)
    embed = proj.shape[0]

    made = permuted(contract_last(sib_rows, proj), sibling)
    others = embedded(both.reshape(N_Y * N_X, -1, width), N_ZH * picked, proj)
    spot = jnp.where(first, y * N_X + x, x * N_Y + y) * (N_ZH * picked)
    at = jnp.stack([sub * picked, spot]).astype(jnp.int32)
    part = partial_grads(at, jnp.stack([scale, shift_by, weight]), made, others, picked)

    terms = contract_first(part, feat).astype(bf16)
    part, terms = lax.optimization_barrier((part, terms))
    terms = exchanged(terms.reshape(N_Y * N_X, embed // (N_Y * N_X), width), PLANE)
    held = part.astype(f32)
    for bit, hop in ((4, 1), (2, 2), (1, 4)):
        count = held.shape[0] // 2
        high = (sub & bit) // bit
        send = lax.dynamic_slice_in_dim(held, (1 - high) * count, count, 0).astype(bf16)
        stay = lax.dynamic_slice_in_dim(held, high * count, count, 0)
        held = stay + permuted(send, along(hop)).astype(f32)
    du, terms, other_proj = lax.optimization_barrier(
        (held.astype(bf16), terms, permuted(proj, sibling))
    )
    for bit, hop in ((1, 4), (2, 2), (4, 1)):
        came = permuted(du, along(hop))
        high = (sub & bit) > 0
        du = jnp.concatenate([jnp.where(high, came, du), jnp.where(high, du, came)], 0)

    terms = jnp.sum(terms.astype(f32), 0)
    lower, upper = terms[:pair], terms[pair:]
    came = permuted(jnp.where(low, upper, lower).astype(bf16), mirror)
    total = (jnp.where(low, lower, upper) + came.astype(f32)).astype(bf16)
    total = (total.astype(f32) + permuted(total, along(4)).astype(f32)).astype(bf16)
    total = summed(total, *(permuted(total, along(hop)) for hop in (1, 2, 3)))
    keep_g = jnp.where(first, total[:cols], total[cols:pair])
    got_g = permuted(jnp.where(first, total[cols:pair], total[:cols]), sibling)
    img_proj_grad = jnp.where(first, got_g, keep_g).T
    txt_proj_grad = jnp.where(first, keep_g, got_g).T

    grad = jnp.dot(du, other_proj, preferred_element_type=f32)
    grad = grad.reshape(N_BLK, N_CORE, sub_rows, width)
    keep_r = grad[:, 0].reshape(rows, width)
    got_r = permuted(grad[:, 1].reshape(rows, width), sibling)
    img_grad = jnp.where(first, got_r, keep_r)
    txt_grad = jnp.where(first, keep_r, got_r)
    return (img_grad, txt_grad, img_proj_grad, txt_proj_grad)


def solution(mesh):
    return jax.shard_map(
        body,
        mesh=mesh,
        in_specs=(P("grp", None), P("grp", None), P(None, "grp"), P(None, "grp"), P(), P(), P()),
        out_specs=(P("grp", None), P("grp", None), P(None, "grp"), P(None, "grp")),
        check_vma=False,
    )
```

```python
import functools

import jax
import jax.numpy as jnp
from jax import lax
from jax.experimental import pallas as pl
from jax.experimental.pallas import tpu as pltpu
from jax.sharding import PartitionSpec as P

BOTH = ("blk", "grp")
N_BLK, N_Y, N_ZH, N_X, N_CORE = 8, 4, 2, 4, 2
N_GRP = N_Y * N_ZH * N_X * N_CORE


def place(blk, y, zh, x, core):
    return blk * N_GRP + ((y * N_ZH + zh) * N_X + x) * N_CORE + core


def parts(device):
    blk, grp = divmod(device, N_GRP)
    grp, core = divmod(grp, N_CORE)
    grp, x = divmod(grp, N_X)
    y, zh = divmod(grp, N_ZH)
    return blk, y, zh, x, core


def sibling(device):
    return device ^ 1


def mirror(device):
    blk, y, zh, x, core = parts(device)
    return place(N_BLK - 1 - blk, y, 1 - zh, x, core)


def along(hop):
    return lambda device: device ^ (hop * N_GRP)


def crossed(first_axis):
    groups = []
    for blk in range(N_BLK):
        for zh in range(N_ZH):
            for core in range(N_CORE):
                along_x = (first_axis == "x") == (core == 0)
                for fixed in range(4):
                    groups.append(
                        [
                            place(blk, fixed, zh, at, core)
                            if along_x
                            else place(blk, at, zh, fixed, core)
                            for at in range(4)
                        ]
                    )
    return groups


INNER, OUTER = crossed("x"), crossed("y")
PLANE = [
    [place(blk, y, zh, x, core) for y in range(N_Y) for x in range(N_X)]
    for blk in range(N_BLK)
    for zh in range(N_ZH)
    for core in range(N_CORE)
]


def permuted(value, target):
    pairs = [(source, target(source)) for source in range(N_BLK * N_GRP)]
    return lax.ppermute(value, BOTH, pairs)


def exchanged(value, groups):
    return lax.all_to_all(value, BOTH, 0, 0, axis_index_groups=groups, tiled=True)


def gathered(value, groups):
    count = len(groups[0])
    copies = jnp.broadcast_to(value[None], (count,) + value.shape)
    return exchanged(copies, groups)


def summed(own, beside, across, both):
    own, beside, across, both = (v.astype(jnp.float32) for v in (own, beside, across, both))
    return (own + beside) + (across + both)


def contract_last(left, right):
    return lax.dot_general(
        left, right, (((1,), (1,)), ((), ())), preferred_element_type=jnp.float32
    )


def contract_first(left, right):
    return lax.dot_general(
        left, right, (((0,), (0,)), ((), ())), preferred_element_type=jnp.float32
    )


def embed_kernel(feat_ref, proj_ref, emb_ref):
    proj_out = contract_last(feat_ref[...].reshape(emb_ref.shape), proj_ref[...])
    inverse = lax.rsqrt(jnp.sum(proj_out * proj_out, axis=1, keepdims=True) + 1e-06)
    emb_ref[...] = (proj_out * inverse).astype(jnp.bfloat16)


def embedded(both, picked, proj):
    count, _, width = both.shape
    embed = proj.shape[0]
    group = 8
    rows = count * picked
    return pl.pallas_call(
        embed_kernel,
        grid=(count // group,),
        in_specs=[
            pl.BlockSpec((group, picked, width), lambda i: (i, 0, 0)),
            pl.BlockSpec((embed, width), lambda i: (0, 0)),
        ],
        out_specs=pl.BlockSpec((group * picked, embed), lambda i: (i, 0)),
        out_shape=jax.ShapeDtypeStruct((rows, embed), jnp.bfloat16),
        compiler_params=pltpu.CompilerParams(vmem_limit_bytes=40 * 2**20),
        cost_estimate=pl.CostEstimate(
            flops=2 * rows * embed * width,
            bytes_accessed=2 * (rows * width + rows * embed + embed * width),
            transcendentals=rows,
        ),
    )(both, proj)


def partial_kernel(at_ref, par_ref, made_ref, others_ref, part_ref, emb_ref, acc_ref, *, block):
    step = pl.program_id(0)
    scale, shift_by, weight = par_ref[0], par_ref[1], par_ref[2]

    def unit_of():
        made = made_ref[...]
        inverse = lax.rsqrt(jnp.sum(made * made, axis=1, keepdims=True) + 1e-06)
        return made * inverse, inverse

    @pl.when(step == 0)
    def _():
        emb_ref[...] = unit_of()[0].astype(jnp.bfloat16)
        acc_ref[...] = jnp.zeros_like(acc_ref)

    others = others_ref[...]
    logits = scale * contract_last(emb_ref[...], others) + shift_by
    row = lax.broadcasted_iota(jnp.int32, logits.shape, 0) - at_ref[0]
    col = lax.broadcasted_iota(jnp.int32, logits.shape, 1) + (step * logits.shape[1] - at_ref[1])
    same = (row == col) & (row >= 0) & (row < block)
    coef = jnp.where(same, -weight, weight) * jax.nn.sigmoid(jnp.where(same, -logits, logits))
    acc_ref[...] += jnp.dot(
        coef.astype(jnp.bfloat16), others, preferred_element_type=jnp.float32
    )

    @pl.when(step == pl.num_programs(0) - 1)
    def _():
        unit, inverse = unit_of()
        grad_unit = scale * acc_ref[...]
        inner = jnp.sum(unit * grad_unit, axis=1, keepdims=True)
        part_ref[...] = ((grad_unit - unit * inner) * inverse).astype(jnp.bfloat16)


def partial_grads(at, params, made, others, block):
    own, embed = made.shape
    count = others.shape[0]
    tile = count
    return pl.pallas_call(
        functools.partial(partial_kernel, block=block),
        grid=(count // tile,),
        in_specs=[
            pl.BlockSpec(memory_space=pltpu.SMEM),
            pl.BlockSpec(memory_space=pltpu.SMEM),
            pl.BlockSpec((own, embed), lambda i: (0, 0)),
            pl.BlockSpec((tile, embed), lambda i: (i, 0)),
        ],
        out_specs=pl.BlockSpec((own, embed), lambda i: (0, 0)),
        out_shape=jax.ShapeDtypeStruct((own, embed), jnp.bfloat16),
        scratch_shapes=[
            pltpu.VMEM((own, embed), jnp.bfloat16),
            pltpu.VMEM((own, embed), jnp.float32),
        ],
        compiler_params=pltpu.CompilerParams(vmem_limit_bytes=40 * 2**20),
        cost_estimate=pl.CostEstimate(
            flops=4 * own * count * embed,
            bytes_accessed=2 * count * embed + 6 * own * embed,
            transcendentals=own * count,
        ),
    )(at, params, made, others)


def body(img_feat, txt_feat, img_proj, txt_proj, logit_scale, logit_bias, loss_weight):
    bf16, f32 = jnp.bfloat16, jnp.float32
    scale, shift_by, weight = logit_scale[0], logit_bias[0], loss_weight[0]
    rows, width = img_feat.shape
    cols = img_proj.shape[1]
    blk = lax.axis_index("blk")
    grp = lax.axis_index("grp")
    core = grp % N_CORE
    x = (grp // N_CORE) % N_X
    zh = (grp // (N_CORE * N_X)) % N_ZH
    y = grp // (N_CORE * N_X * N_ZH)
    first = core == 0
    steps = jnp.where(zh == 0, blk, N_BLK - 1 - blk)
    sub = (steps & 1) * 4 + (steps & 2) + (steps & 4) // 4
    sub_rows = rows // N_BLK
    own = N_CORE * rows

    low = zh == 0
    img_t, txt_t = img_proj.T, txt_proj.T
    own_f, other_f = jnp.where(first, img_feat, txt_feat), jnp.where(first, txt_feat, img_feat)
    own_sub = lax.dynamic_slice_in_dim(own_f, sub * sub_rows, sub_rows, 0)
    other_sub = lax.dynamic_slice_in_dim(other_f, sub * sub_rows, sub_rows, 0)
    ours = jnp.concatenate([own_sub, jnp.where(first, img_t, txt_t)], 0)
    theirs = jnp.concatenate([other_sub, jnp.where(first, txt_t, img_t)], 0)

    def joined(mine, siblings):
        mine_t, siblings_t = mine[sub_rows:], siblings[sub_rows:]
        return jnp.concatenate(
            [
                mine[:sub_rows],
                siblings[:sub_rows],
                jnp.where(first, mine_t, siblings_t),
                jnp.where(first, siblings_t, mine_t),
            ],
            0,
        )

    far = joined(
        permuted(ours, mirror), permuted(theirs, lambda device: mirror(sibling(device)))
    )
    near = gathered(joined(ours, permuted(theirs, sibling)), INNER)
    far = gathered(far, INNER)
    picked = N_CORE * sub_rows
    pair = N_CORE * cols
    both = jnp.concatenate(
        [
            near[:, :picked],
            far[:, :picked],
            jnp.where(low, near[:, picked:], far[:, picked:]),
            jnp.where(low, far[:, picked:], near[:, picked:]),
        ],
        1,
    )
    sib_feat = permuted(jnp.concatenate([own_f, other_f], 0), sibling)
    sib_other, sib_own = sib_feat[:rows], sib_feat[rows:]

    def interleaved(one, two):
        shape = (N_BLK, sub_rows, width)
        return jnp.stack([one.reshape(shape), two.reshape(shape)], 1).reshape(own, width)

    feat = interleaved(other_f, sib_other)
    sib_rows = interleaved(sib_own, own_f)
    both, feat, sib_rows = lax.optimization_barrier((both, feat, sib_rows))

    both = gathered(both, OUTER)
    proj = both[:, :, N_ZH * picked :]
    proj = jnp.where(first, proj, proj.transpose(1, 0, 2, 3)).reshape(-1, width)
    embed = proj.shape[0]

    made = permuted(contract_last(sib_rows, proj), sibling)
    others = embedded(both.reshape(N_Y * N_X, -1, width), N_ZH * picked, proj)
    spot = jnp.where(first, y * N_X + x, x * N_Y + y) * (N_ZH * picked)
    at = jnp.stack([sub * picked, spot]).astype(jnp.int32)
    part = partial_grads(at, jnp.stack([scale, shift_by, weight]), made, others, picked)

    terms = contract_first(part, feat).astype(bf16)
    part, terms, late_proj = lax.optimization_barrier((part, terms, proj))
    terms = exchanged(terms.reshape(N_Y * N_X, embed // (N_Y * N_X), width), PLANE)
    quarter = own // 4
    at_quarter = sub // 2

    def quarter_of(index):
        return lax.dynamic_slice_in_dim(part, index * quarter, quarter, 0)

    held = summed(
        quarter_of(at_quarter),
        permuted(quarter_of(at_quarter ^ 2), along(1)),
        permuted(quarter_of(at_quarter ^ 1), along(2)),
        permuted(quarter_of(at_quarter ^ 3), along(3)),
    ).astype(bf16)
    held = held.astype(f32) + permuted(held, along(4)).astype(f32)
    du, terms, other_proj = lax.optimization_barrier(
        (held.astype(bf16), terms, permuted(late_proj, sibling))
    )
    pieces = [du] + [permuted(du, along(hop)) for hop in (2, 1, 3)]
    swap = (at_quarter & 1) == 1
    pieces = [jnp.where(swap, pieces[index ^ 1], pieces[index]) for index in range(4)]
    swap = (at_quarter & 2) == 2
    pieces = [jnp.where(swap, pieces[index ^ 2], pieces[index]) for index in range(4)]
    du = jnp.concatenate(pieces, 0)

    terms = jnp.sum(terms.astype(f32), 0)
    lower, upper = terms[:pair], terms[pair:]
    came = permuted(jnp.where(low, upper, lower).astype(bf16), mirror)
    total = (jnp.where(low, lower, upper) + came.astype(f32)).astype(bf16)
    total = (total.astype(f32) + permuted(total, along(4)).astype(f32)).astype(bf16)
    total = summed(total, *(permuted(total, along(hop)) for hop in (1, 2, 3)))
    keep_g = jnp.where(first, total[:cols], total[cols:pair])
    got_g = permuted(jnp.where(first, total[cols:pair], total[:cols]), sibling)
    img_proj_grad = jnp.where(first, got_g, keep_g).T
    txt_proj_grad = jnp.where(first, keep_g, got_g).T

    grad = jnp.dot(du, other_proj, preferred_element_type=f32)
    grad = grad.reshape(N_BLK, N_CORE, sub_rows, width)
    keep_r = grad[:, 0].reshape(rows, width)
    got_r = permuted(grad[:, 1].reshape(rows, width), sibling)
    img_grad = jnp.where(first, got_r, keep_r)
    txt_grad = jnp.where(first, keep_r, got_r)
    return (img_grad, txt_grad, img_proj_grad, txt_proj_grad)


def solution(mesh):
    return jax.shard_map(
        body,
        mesh=mesh,
        in_specs=(P("grp", None), P("grp", None), P(None, "grp"), P(None, "grp"), P(), P(), P()),
        out_specs=(P("grp", None), P("grp", None), P(None, "grp"), P(None, "grp")),
        check_vma=False,
    )
```

```python
import functools

import jax
import jax.numpy as jnp
from jax import lax
from jax.experimental import pallas as pl
from jax.experimental.pallas import tpu as pltpu
from jax.sharding import PartitionSpec as P

BOTH = ("blk", "grp")
N_BLK, N_Y, N_ZH, N_X, N_CORE = 8, 4, 2, 4, 2
N_GRP = N_Y * N_ZH * N_X * N_CORE


def place(blk, y, zh, x, core):
    return blk * N_GRP + ((y * N_ZH + zh) * N_X + x) * N_CORE + core


def parts(device):
    blk, grp = divmod(device, N_GRP)
    grp, core = divmod(grp, N_CORE)
    grp, x = divmod(grp, N_X)
    y, zh = divmod(grp, N_ZH)
    return blk, y, zh, x, core


def sibling(device):
    return device ^ 1


def mirror(device):
    blk, y, zh, x, core = parts(device)
    return place(N_BLK - 1 - blk, y, 1 - zh, x, core)


def along(hop):
    return lambda device: device ^ (hop * N_GRP)


def crossed(first_axis):
    groups = []
    for blk in range(N_BLK):
        for zh in range(N_ZH):
            for core in range(N_CORE):
                along_x = (first_axis == "x") == (core == 0)
                for fixed in range(4):
                    groups.append(
                        [
                            place(blk, fixed, zh, at, core)
                            if along_x
                            else place(blk, at, zh, fixed, core)
                            for at in range(4)
                        ]
                    )
    return groups


INNER, OUTER = crossed("x"), crossed("y")
PLANE = [
    [place(blk, y, zh, x, core) for y in range(N_Y) for x in range(N_X)]
    for blk in range(N_BLK)
    for zh in range(N_ZH)
    for core in range(N_CORE)
]


def permuted(value, target):
    pairs = [(source, target(source)) for source in range(N_BLK * N_GRP)]
    return lax.ppermute(value, BOTH, pairs)


def exchanged(value, groups):
    return lax.all_to_all(value, BOTH, 0, 0, axis_index_groups=groups, tiled=True)


def gathered(value, groups):
    count = len(groups[0])
    copies = jnp.broadcast_to(value[None], (count,) + value.shape)
    return exchanged(copies, groups)


def summed(own, beside, across, both):
    own, beside, across, both = (v.astype(jnp.float32) for v in (own, beside, across, both))
    return (own + beside) + (across + both)


def contract_last(left, right):
    return lax.dot_general(
        left, right, (((1,), (1,)), ((), ())), preferred_element_type=jnp.float32
    )


def contract_first(left, right):
    return lax.dot_general(
        left, right, (((0,), (0,)), ((), ())), preferred_element_type=jnp.float32
    )


def embed_kernel(feat_ref, proj_ref, emb_ref):
    proj_out = contract_last(feat_ref[...].reshape(emb_ref.shape), proj_ref[...])
    inverse = lax.rsqrt(jnp.sum(proj_out * proj_out, axis=1, keepdims=True) + 1e-06)
    emb_ref[...] = (proj_out * inverse).astype(jnp.bfloat16)


def embedded(both, picked, proj):
    count, _, width = both.shape
    embed = proj.shape[0]
    group = 8
    rows = count * picked
    return pl.pallas_call(
        embed_kernel,
        grid=(count // group,),
        in_specs=[
            pl.BlockSpec((group, picked, width), lambda i: (i, 0, 0)),
            pl.BlockSpec((embed, width), lambda i: (0, 0)),
        ],
        out_specs=pl.BlockSpec((group * picked, embed), lambda i: (i, 0)),
        out_shape=jax.ShapeDtypeStruct((rows, embed), jnp.bfloat16),
        compiler_params=pltpu.CompilerParams(vmem_limit_bytes=20 * 2**20),
        cost_estimate=pl.CostEstimate(
            flops=2 * rows * embed * width,
            bytes_accessed=2 * (rows * width + rows * embed + embed * width),
            transcendentals=rows,
        ),
    )(both, proj)


def partial_kernel(at_ref, par_ref, made_ref, others_ref, part_ref, emb_ref, acc_ref, *, block):
    step = pl.program_id(0)
    scale, shift_by, weight = par_ref[0], par_ref[1], par_ref[2]

    def unit_of():
        made = made_ref[...]
        inverse = lax.rsqrt(jnp.sum(made * made, axis=1, keepdims=True) + 1e-06)
        return made * inverse, inverse

    @pl.when(step == 0)
    def _():
        emb_ref[...] = unit_of()[0].astype(jnp.bfloat16)
        acc_ref[...] = jnp.zeros_like(acc_ref)

    others = others_ref[...]
    logits = scale * contract_last(emb_ref[...], others) + shift_by
    row = lax.broadcasted_iota(jnp.int32, logits.shape, 0) - at_ref[0]
    col = lax.broadcasted_iota(jnp.int32, logits.shape, 1) + (step * logits.shape[1] - at_ref[1])
    same = (row == col) & (row >= 0) & (row < block)
    coef = jnp.where(same, -weight, weight) * jax.nn.sigmoid(jnp.where(same, -logits, logits))
    acc_ref[...] += jnp.dot(
        coef.astype(jnp.bfloat16), others, preferred_element_type=jnp.float32
    )

    @pl.when(step == pl.num_programs(0) - 1)
    def _():
        unit, inverse = unit_of()
        grad_unit = scale * acc_ref[...]
        inner = jnp.sum(unit * grad_unit, axis=1, keepdims=True)
        part_ref[...] = ((grad_unit - unit * inner) * inverse).astype(jnp.bfloat16)


def partial_grads(at, params, made, others, block):
    own, embed = made.shape
    count = others.shape[0]
    tile = count
    return pl.pallas_call(
        functools.partial(partial_kernel, block=block),
        grid=(count // tile,),
        in_specs=[
            pl.BlockSpec(memory_space=pltpu.SMEM),
            pl.BlockSpec(memory_space=pltpu.SMEM),
            pl.BlockSpec((own, embed), lambda i: (0, 0)),
            pl.BlockSpec((tile, embed), lambda i: (i, 0)),
        ],
        out_specs=pl.BlockSpec((own, embed), lambda i: (0, 0)),
        out_shape=jax.ShapeDtypeStruct((own, embed), jnp.bfloat16),
        scratch_shapes=[
            pltpu.VMEM((own, embed), jnp.bfloat16),
            pltpu.VMEM((own, embed), jnp.float32),
        ],
        compiler_params=pltpu.CompilerParams(vmem_limit_bytes=20 * 2**20),
        cost_estimate=pl.CostEstimate(
            flops=4 * own * count * embed,
            bytes_accessed=2 * count * embed + 6 * own * embed,
            transcendentals=own * count,
        ),
    )(at, params, made, others)


def body(img_feat, txt_feat, img_proj, txt_proj, logit_scale, logit_bias, loss_weight):
    bf16, f32 = jnp.bfloat16, jnp.float32
    scale, shift_by, weight = logit_scale[0], logit_bias[0], loss_weight[0]
    rows, width = img_feat.shape
    cols = img_proj.shape[1]
    blk = lax.axis_index("blk")
    grp = lax.axis_index("grp")
    core = grp % N_CORE
    x = (grp // N_CORE) % N_X
    zh = (grp // (N_CORE * N_X)) % N_ZH
    y = grp // (N_CORE * N_X * N_ZH)
    first = core == 0
    steps = jnp.where(zh == 0, blk, N_BLK - 1 - blk)
    sub = (steps & 1) * 4 + (steps & 2) + (steps & 4) // 4
    sub_rows = rows // N_BLK
    own = N_CORE * rows

    low = zh == 0
    img_t, txt_t = img_proj.T, txt_proj.T
    own_f, other_f = jnp.where(first, img_feat, txt_feat), jnp.where(first, txt_feat, img_feat)
    own_sub = lax.dynamic_slice_in_dim(own_f, sub * sub_rows, sub_rows, 0)
    other_sub = lax.dynamic_slice_in_dim(other_f, sub * sub_rows, sub_rows, 0)
    ours = jnp.concatenate([own_sub, jnp.where(first, img_t, txt_t)], 0)
    theirs = jnp.concatenate([other_sub, jnp.where(first, txt_t, img_t)], 0)

    def joined(mine, siblings):
        mine_t, siblings_t = mine[sub_rows:], siblings[sub_rows:]
        return jnp.concatenate(
            [
                mine[:sub_rows],
                siblings[:sub_rows],
                jnp.where(first, mine_t, siblings_t),
                jnp.where(first, siblings_t, mine_t),
            ],
            0,
        )

    far = joined(
        permuted(ours, mirror), permuted(theirs, lambda device: mirror(sibling(device)))
    )
    near = gathered(joined(ours, permuted(theirs, sibling)), INNER)
    far = gathered(far, INNER)
    picked = N_CORE * sub_rows
    pair = N_CORE * cols
    both = jnp.concatenate(
        [
            near[:, :picked],
            far[:, :picked],
            jnp.where(low, near[:, picked:], far[:, picked:]),
            jnp.where(low, far[:, picked:], near[:, picked:]),
        ],
        1,
    )
    sib_feat = permuted(jnp.concatenate([own_f, other_f], 0), sibling)
    sib_other, sib_own = sib_feat[:rows], sib_feat[rows:]

    def interleaved(one, two):
        shape = (N_BLK, sub_rows, width)
        return jnp.stack([one.reshape(shape), two.reshape(shape)], 1).reshape(own, width)

    feat = interleaved(other_f, sib_other)
    sib_rows = interleaved(sib_own, own_f)
    both, feat, sib_rows = lax.optimization_barrier((both, feat, sib_rows))

    both = gathered(both, OUTER)
    proj = both[:, :, N_ZH * picked :]
    proj = jnp.where(first, proj, proj.transpose(1, 0, 2, 3)).reshape(-1, width)
    embed = proj.shape[0]

    made = permuted(contract_last(sib_rows, proj), sibling)
    others = embedded(both.reshape(N_Y * N_X, -1, width), N_ZH * picked, proj)
    spot = jnp.where(first, y * N_X + x, x * N_Y + y) * (N_ZH * picked)
    at = jnp.stack([sub * picked, spot]).astype(jnp.int32)
    part = partial_grads(at, jnp.stack([scale, shift_by, weight]), made, others, picked)

    terms = contract_first(part, feat).astype(bf16)
    part, terms, late_proj = lax.optimization_barrier((part, terms, proj))
    terms = exchanged(terms.reshape(N_Y * N_X, embed // (N_Y * N_X), width), PLANE)
    quarter = own // 4
    at_quarter = sub // 2

    def quarter_of(index):
        return lax.dynamic_slice_in_dim(part, index * quarter, quarter, 0)

    held = summed(
        quarter_of(at_quarter),
        permuted(quarter_of(at_quarter ^ 2), along(1)),
        permuted(quarter_of(at_quarter ^ 1), along(2)),
        permuted(quarter_of(at_quarter ^ 3), along(3)),
    ).astype(bf16)
    held, late_proj = lax.optimization_barrier((held, late_proj))
    held = held.astype(f32) + permuted(held, along(4)).astype(f32)
    terms = jnp.sum(terms.astype(f32), 0)
    lower, upper = terms[:pair], terms[pair:]
    came = permuted(jnp.where(low, upper, lower).astype(bf16), mirror)
    du, came, other_proj = lax.optimization_barrier(
        (held.astype(bf16), came, permuted(late_proj, sibling))
    )
    pieces = [du] + [permuted(du, along(hop)) for hop in (2, 1, 3)]
    swap = (at_quarter & 1) == 1
    pieces = [jnp.where(swap, pieces[index ^ 1], pieces[index]) for index in range(4)]
    swap = (at_quarter & 2) == 2
    pieces = [jnp.where(swap, pieces[index ^ 2], pieces[index]) for index in range(4)]
    du = jnp.concatenate(pieces, 0)

    total = (jnp.where(low, lower, upper) + came.astype(f32)).astype(bf16)
    total = (total.astype(f32) + permuted(total, along(4)).astype(f32)).astype(bf16)
    total = summed(total, *(permuted(total, along(hop)) for hop in (1, 2, 3)))
    keep_g = jnp.where(first, total[:cols], total[cols:pair])
    got_g = permuted(jnp.where(first, total[cols:pair], total[:cols]), sibling)
    img_proj_grad = jnp.where(first, got_g, keep_g).T
    txt_proj_grad = jnp.where(first, keep_g, got_g).T

    grad = jnp.dot(du, other_proj, preferred_element_type=f32)
    grad = grad.reshape(N_BLK, N_CORE, sub_rows, width)
    keep_r = grad[:, 0].reshape(rows, width)
    got_r = permuted(grad[:, 1].reshape(rows, width), sibling)
    img_grad = jnp.where(first, got_r, keep_r)
    txt_grad = jnp.where(first, keep_r, got_r)
    return (img_grad, txt_grad, img_proj_grad, txt_proj_grad)


def solution(mesh):
    return jax.shard_map(
        body,
        mesh=mesh,
        in_specs=(P("grp", None), P("grp", None), P(None, "grp"), P(None, "grp"), P(), P(), P()),
        out_specs=(P("grp", None), P("grp", None), P(None, "grp"), P(None, "grp")),
        check_vma=False,
    )
```

```python
import functools

import jax
import jax.numpy as jnp
from jax import lax
from jax.experimental import pallas as pl
from jax.experimental.pallas import tpu as pltpu
from jax.sharding import PartitionSpec as P

BOTH = ("blk", "grp")
N_BLK, N_Y, N_ZH, N_X, N_CORE = 8, 4, 2, 4, 2
N_GRP = N_Y * N_ZH * N_X * N_CORE


def place(blk, y, zh, x, core):
    return blk * N_GRP + ((y * N_ZH + zh) * N_X + x) * N_CORE + core


def parts(device):
    blk, grp = divmod(device, N_GRP)
    grp, core = divmod(grp, N_CORE)
    grp, x = divmod(grp, N_X)
    y, zh = divmod(grp, N_ZH)
    return blk, y, zh, x, core


def sibling(device):
    return device ^ 1


def mirror(device):
    blk, y, zh, x, core = parts(device)
    return place(N_BLK - 1 - blk, y, 1 - zh, x, core)


def along(hop):
    return lambda device: device ^ (hop * N_GRP)


def crossed(first_axis):
    groups = []
    for blk in range(N_BLK):
        for zh in range(N_ZH):
            for core in range(N_CORE):
                along_x = (first_axis == "x") == (core == 0)
                for fixed in range(4):
                    groups.append(
                        [
                            place(blk, fixed, zh, at, core)
                            if along_x
                            else place(blk, at, zh, fixed, core)
                            for at in range(4)
                        ]
                    )
    return groups


INNER, OUTER = crossed("x"), crossed("y")


def permuted(value, target):
    pairs = [(source, target(source)) for source in range(N_BLK * N_GRP)]
    return lax.ppermute(value, BOTH, pairs)


def exchanged(value, groups):
    return lax.all_to_all(value, BOTH, 0, 0, axis_index_groups=groups, tiled=True)


def gathered(value, groups):
    count = len(groups[0])
    copies = jnp.broadcast_to(value[None], (count,) + value.shape)
    return exchanged(copies, groups)


def summed(own, beside, across, both):
    own, beside, across, both = (v.astype(jnp.float32) for v in (own, beside, across, both))
    return (own + beside) + (across + both)


def contract_last(left, right):
    return lax.dot_general(
        left, right, (((1,), (1,)), ((), ())), preferred_element_type=jnp.float32
    )


def contract_first(left, right):
    return lax.dot_general(
        left, right, (((0,), (0,)), ((), ())), preferred_element_type=jnp.float32
    )


def embed_kernel(feat_ref, proj_ref, emb_ref):
    proj_out = contract_last(feat_ref[...].reshape(emb_ref.shape), proj_ref[...])
    inverse = lax.rsqrt(jnp.sum(proj_out * proj_out, axis=1, keepdims=True) + 1e-06)
    emb_ref[...] = (proj_out * inverse).astype(jnp.bfloat16)


def embedded(both, picked, proj):
    count, _, width = both.shape
    embed = proj.shape[0]
    group = 8
    rows = count * picked
    return pl.pallas_call(
        embed_kernel,
        grid=(count // group,),
        in_specs=[
            pl.BlockSpec((group, picked, width), lambda i: (i, 0, 0)),
            pl.BlockSpec((embed, width), lambda i: (0, 0)),
        ],
        out_specs=pl.BlockSpec((group * picked, embed), lambda i: (i, 0)),
        out_shape=jax.ShapeDtypeStruct((rows, embed), jnp.bfloat16),
        compiler_params=pltpu.CompilerParams(vmem_limit_bytes=20 * 2**20),
        cost_estimate=pl.CostEstimate(
            flops=2 * rows * embed * width,
            bytes_accessed=2 * (rows * width + rows * embed + embed * width),
            transcendentals=rows,
        ),
    )(both, proj)


def partial_kernel(at_ref, par_ref, made_ref, others_ref, part_ref, emb_ref, acc_ref, *, block):
    step = pl.program_id(0)
    scale, shift_by, weight = par_ref[0], par_ref[1], par_ref[2]

    def unit_of():
        made = made_ref[...]
        inverse = lax.rsqrt(jnp.sum(made * made, axis=1, keepdims=True) + 1e-06)
        return made * inverse, inverse

    @pl.when(step == 0)
    def _():
        emb_ref[...] = unit_of()[0].astype(jnp.bfloat16)
        acc_ref[...] = jnp.zeros_like(acc_ref)

    others = others_ref[...]
    logits = scale * contract_last(emb_ref[...], others) + shift_by
    row = lax.broadcasted_iota(jnp.int32, logits.shape, 0) - at_ref[0]
    col = lax.broadcasted_iota(jnp.int32, logits.shape, 1) + (step * logits.shape[1] - at_ref[1])
    same = (row == col) & (row >= 0) & (row < block)
    coef = jnp.where(same, -weight, weight) * jax.nn.sigmoid(jnp.where(same, -logits, logits))
    acc_ref[...] += jnp.dot(
        coef.astype(jnp.bfloat16), others, preferred_element_type=jnp.float32
    )

    @pl.when(step == pl.num_programs(0) - 1)
    def _():
        unit, inverse = unit_of()
        grad_unit = scale * acc_ref[...]
        inner = jnp.sum(unit * grad_unit, axis=1, keepdims=True)
        part_ref[...] = ((grad_unit - unit * inner) * inverse).astype(jnp.bfloat16)


def partial_grads(at, params, made, others, block):
    own, embed = made.shape
    count = others.shape[0]
    tile = count
    return pl.pallas_call(
        functools.partial(partial_kernel, block=block),
        grid=(count // tile,),
        in_specs=[
            pl.BlockSpec(memory_space=pltpu.SMEM),
            pl.BlockSpec(memory_space=pltpu.SMEM),
            pl.BlockSpec((own, embed), lambda i: (0, 0)),
            pl.BlockSpec((tile, embed), lambda i: (i, 0)),
        ],
        out_specs=pl.BlockSpec((own, embed), lambda i: (0, 0)),
        out_shape=jax.ShapeDtypeStruct((own, embed), jnp.bfloat16),
        scratch_shapes=[
            pltpu.VMEM((own, embed), jnp.bfloat16),
            pltpu.VMEM((own, embed), jnp.float32),
        ],
        compiler_params=pltpu.CompilerParams(vmem_limit_bytes=20 * 2**20),
        cost_estimate=pl.CostEstimate(
            flops=4 * own * count * embed,
            bytes_accessed=2 * count * embed + 6 * own * embed,
            transcendentals=own * count,
        ),
    )(at, params, made, others)


def body(img_feat, txt_feat, img_proj, txt_proj, logit_scale, logit_bias, loss_weight):
    bf16, f32 = jnp.bfloat16, jnp.float32
    scale, shift_by, weight = logit_scale[0], logit_bias[0], loss_weight[0]
    rows, width = img_feat.shape
    cols = img_proj.shape[1]
    blk = lax.axis_index("blk")
    grp = lax.axis_index("grp")
    core = grp % N_CORE
    x = (grp // N_CORE) % N_X
    zh = (grp // (N_CORE * N_X)) % N_ZH
    y = grp // (N_CORE * N_X * N_ZH)
    first = core == 0
    steps = jnp.where(zh == 0, blk, N_BLK - 1 - blk)
    sub = (steps & 1) * 4 + (steps & 2) + (steps & 4) // 4
    sub_rows = rows // N_BLK
    own = N_CORE * rows

    low = zh == 0
    img_t, txt_t = img_proj.T, txt_proj.T
    own_f, other_f = jnp.where(first, img_feat, txt_feat), jnp.where(first, txt_feat, img_feat)
    own_sub = lax.dynamic_slice_in_dim(own_f, sub * sub_rows, sub_rows, 0)
    other_sub = lax.dynamic_slice_in_dim(other_f, sub * sub_rows, sub_rows, 0)
    ours = jnp.concatenate([own_sub, jnp.where(first, img_t, txt_t)], 0)
    theirs = jnp.concatenate([other_sub, jnp.where(first, txt_t, img_t)], 0)

    def joined(mine, siblings):
        mine_t, siblings_t = mine[sub_rows:], siblings[sub_rows:]
        return jnp.concatenate(
            [
                mine[:sub_rows],
                siblings[:sub_rows],
                jnp.where(first, mine_t, siblings_t),
                jnp.where(first, siblings_t, mine_t),
            ],
            0,
        )

    far = joined(
        permuted(ours, mirror), permuted(theirs, lambda device: mirror(sibling(device)))
    )
    near = gathered(joined(ours, permuted(theirs, sibling)), INNER)
    far = gathered(far, INNER)
    picked = N_CORE * sub_rows
    pair = N_CORE * cols
    both = jnp.concatenate(
        [
            near[:, :picked],
            far[:, :picked],
            jnp.where(low, near[:, picked:], far[:, picked:]),
            jnp.where(low, far[:, picked:], near[:, picked:]),
        ],
        1,
    )
    sib_feat = permuted(jnp.concatenate([own_f, other_f], 0), sibling)
    sib_other, sib_own = sib_feat[:rows], sib_feat[rows:]

    def interleaved(one, two):
        shape = (N_BLK, sub_rows, width)
        return jnp.stack([one.reshape(shape), two.reshape(shape)], 1).reshape(own, width)

    feat = interleaved(other_f, sib_other)
    sib_rows = interleaved(sib_own, own_f)
    both, feat, sib_rows = lax.optimization_barrier((both, feat, sib_rows))

    both = gathered(both, OUTER)
    proj = both[:, :, N_ZH * picked :]
    flipped = proj.transpose(1, 0, 2, 3).reshape(-1, width)
    proj = proj.reshape(-1, width)
    embed = proj.shape[0]

    made = permuted(contract_last(sib_rows, flipped), sibling)
    others = embedded(both.reshape(N_Y * N_X, -1, width), N_ZH * picked, proj)
    spot = jnp.where(first, y * N_X + x, x * N_Y + y) * (N_ZH * picked)
    at = jnp.stack([sub * picked, spot]).astype(jnp.int32)
    part = partial_grads(at, jnp.stack([scale, shift_by, weight]), made, others, picked)

    terms = contract_first(part, feat).astype(bf16)
    part, terms, late_proj = lax.optimization_barrier((part, terms, flipped))
    terms = exchanged(terms.reshape(4, embed // 4, width), OUTER)
    terms = jnp.sum(terms.astype(f32), 0).astype(bf16)
    quarter = own // 4
    at_quarter = sub // 2

    def quarter_of(index):
        return lax.dynamic_slice_in_dim(part, index * quarter, quarter, 0)

    held = summed(
        quarter_of(at_quarter),
        permuted(quarter_of(at_quarter ^ 2), along(1)),
        permuted(quarter_of(at_quarter ^ 1), along(2)),
        permuted(quarter_of(at_quarter ^ 3), along(3)),
    ).astype(bf16)
    held, terms, late_proj = lax.optimization_barrier((held, terms, late_proj))
    terms = exchanged(terms.reshape(4, embed // 16, width), INNER)
    held = held.astype(f32) + permuted(held, along(4)).astype(f32)
    terms = jnp.sum(terms.astype(f32), 0)
    lower, upper = terms[:pair], terms[pair:]
    came = permuted(jnp.where(low, upper, lower).astype(bf16), mirror)
    du, came, other_proj = lax.optimization_barrier(
        (held.astype(bf16), came, permuted(late_proj, sibling))
    )
    pieces = [du] + [permuted(du, along(hop)) for hop in (2, 1, 3)]
    swap = (at_quarter & 1) == 1
    pieces = [jnp.where(swap, pieces[index ^ 1], pieces[index]) for index in range(4)]
    swap = (at_quarter & 2) == 2
    pieces = [jnp.where(swap, pieces[index ^ 2], pieces[index]) for index in range(4)]
    du = jnp.concatenate(pieces, 0)

    total = (jnp.where(low, lower, upper) + came.astype(f32)).astype(bf16)
    total = (total.astype(f32) + permuted(total, along(4)).astype(f32)).astype(bf16)
    total = summed(total, *(permuted(total, along(hop)) for hop in (1, 2, 3)))
    keep_g = jnp.where(first, total[:cols], total[cols:pair])
    got_g = permuted(jnp.where(first, total[cols:pair], total[:cols]), sibling)
    img_proj_grad = jnp.where(first, got_g, keep_g).T
    txt_proj_grad = jnp.where(first, keep_g, got_g).T

    grad = jnp.dot(du, other_proj, preferred_element_type=f32)
    grad = grad.reshape(N_BLK, N_CORE, sub_rows, width)
    keep_r = grad[:, 0].reshape(rows, width)
    got_r = permuted(grad[:, 1].reshape(rows, width), sibling)
    img_grad = jnp.where(first, got_r, keep_r)
    txt_grad = jnp.where(first, keep_r, got_r)
    return (img_grad, txt_grad, img_proj_grad, txt_proj_grad)


def solution(mesh):
    return jax.shard_map(
        body,
        mesh=mesh,
        in_specs=(P("grp", None), P("grp", None), P(None, "grp"), P(None, "grp"), P(), P(), P()),
        out_specs=(P("grp", None), P("grp", None), P(None, "grp"), P(None, "grp")),
        check_vma=False,
    )
```

```python
import functools

import jax
import jax.numpy as jnp
from jax import lax
from jax.experimental import pallas as pl
from jax.experimental.pallas import tpu as pltpu
from jax.sharding import PartitionSpec as P

BOTH = ("blk", "grp")
N_BLK, N_Y, N_ZH, N_X, N_CORE = 8, 4, 2, 4, 2
N_GRP = N_Y * N_ZH * N_X * N_CORE


def place(blk, y, zh, x, core):
    return blk * N_GRP + ((y * N_ZH + zh) * N_X + x) * N_CORE + core


def parts(device):
    blk, grp = divmod(device, N_GRP)
    grp, core = divmod(grp, N_CORE)
    grp, x = divmod(grp, N_X)
    y, zh = divmod(grp, N_ZH)
    return blk, y, zh, x, core


def sibling(device):
    return device ^ 1


def mirror(device):
    blk, y, zh, x, core = parts(device)
    return place(N_BLK - 1 - blk, y, 1 - zh, x, core)


def along(hop):
    return lambda device: device ^ (hop * N_GRP)


def crossed(first_axis):
    groups = []
    for blk in range(N_BLK):
        for zh in range(N_ZH):
            for core in range(N_CORE):
                along_x = (first_axis == "x") == (core == 0)
                for fixed in range(4):
                    groups.append(
                        [
                            place(blk, fixed, zh, at, core)
                            if along_x
                            else place(blk, at, zh, fixed, core)
                            for at in range(4)
                        ]
                    )
    return groups


INNER, OUTER = crossed("x"), crossed("y")


def permuted(value, target):
    pairs = [(source, target(source)) for source in range(N_BLK * N_GRP)]
    return lax.ppermute(value, BOTH, pairs)


def exchanged(value, groups):
    return lax.all_to_all(value, BOTH, 0, 0, axis_index_groups=groups, tiled=True)


def gathered(value, groups):
    count = len(groups[0])
    copies = jnp.broadcast_to(value[None], (count,) + value.shape)
    return exchanged(copies, groups)


def summed(own, beside, across, both):
    own, beside, across, both = (v.astype(jnp.float32) for v in (own, beside, across, both))
    return (own + beside) + (across + both)


def contract_last(left, right):
    return lax.dot_general(
        left, right, (((1,), (1,)), ((), ())), preferred_element_type=jnp.float32
    )


def contract_first(left, right):
    return lax.dot_general(
        left, right, (((0,), (0,)), ((), ())), preferred_element_type=jnp.float32
    )


def embed_kernel(feat_ref, proj_ref, emb_ref):
    proj_out = contract_last(feat_ref[...].reshape(emb_ref.shape), proj_ref[...])
    inverse = lax.rsqrt(jnp.sum(proj_out * proj_out, axis=1, keepdims=True) + 1e-06)
    emb_ref[...] = (proj_out * inverse).astype(jnp.bfloat16)


def embedded(both, picked, proj):
    count, _, width = both.shape
    embed = proj.shape[0]
    group = 8
    rows = count * picked
    return pl.pallas_call(
        embed_kernel,
        grid=(count // group,),
        in_specs=[
            pl.BlockSpec((group, picked, width), lambda i: (i, 0, 0)),
            pl.BlockSpec((embed, width), lambda i: (0, 0)),
        ],
        out_specs=pl.BlockSpec((group * picked, embed), lambda i: (i, 0)),
        out_shape=jax.ShapeDtypeStruct((rows, embed), jnp.bfloat16),
        compiler_params=pltpu.CompilerParams(vmem_limit_bytes=20 * 2**20),
        cost_estimate=pl.CostEstimate(
            flops=2 * rows * embed * width,
            bytes_accessed=2 * (rows * width + rows * embed + embed * width),
            transcendentals=rows,
        ),
    )(both, proj)


def partial_kernel(at_ref, par_ref, made_ref, others_ref, part_ref, emb_ref, acc_ref, *, block):
    step = pl.program_id(0)
    scale, shift_by, weight = par_ref[0], par_ref[1], par_ref[2]

    def unit_of():
        made = made_ref[...]
        inverse = lax.rsqrt(jnp.sum(made * made, axis=1, keepdims=True) + 1e-06)
        return made * inverse, inverse

    @pl.when(step == 0)
    def _():
        emb_ref[...] = unit_of()[0].astype(jnp.bfloat16)
        acc_ref[...] = jnp.zeros_like(acc_ref)

    others = others_ref[...]
    logits = scale * contract_last(emb_ref[...], others) + shift_by
    row = lax.broadcasted_iota(jnp.int32, logits.shape, 0) - at_ref[0]
    col = lax.broadcasted_iota(jnp.int32, logits.shape, 1) + (step * logits.shape[1] - at_ref[1])
    same = (row == col) & (row >= 0) & (row < block)
    coef = jnp.where(same, -weight, weight) * jax.nn.sigmoid(jnp.where(same, -logits, logits))
    acc_ref[...] += jnp.dot(
        coef.astype(jnp.bfloat16), others, preferred_element_type=jnp.float32
    )

    @pl.when(step == pl.num_programs(0) - 1)
    def _():
        unit, inverse = unit_of()
        grad_unit = scale * acc_ref[...]
        inner = jnp.sum(unit * grad_unit, axis=1, keepdims=True)
        part_ref[...] = ((grad_unit - unit * inner) * inverse).astype(jnp.bfloat16)


def partial_grads(at, params, made, others, block):
    own, embed = made.shape
    count = others.shape[0]
    tile = count
    return pl.pallas_call(
        functools.partial(partial_kernel, block=block),
        grid=(count // tile,),
        in_specs=[
            pl.BlockSpec(memory_space=pltpu.SMEM),
            pl.BlockSpec(memory_space=pltpu.SMEM),
            pl.BlockSpec((own, embed), lambda i: (0, 0)),
            pl.BlockSpec((tile, embed), lambda i: (i, 0)),
        ],
        out_specs=pl.BlockSpec((own, embed), lambda i: (0, 0)),
        out_shape=jax.ShapeDtypeStruct((own, embed), jnp.bfloat16),
        scratch_shapes=[
            pltpu.VMEM((own, embed), jnp.bfloat16),
            pltpu.VMEM((own, embed), jnp.float32),
        ],
        compiler_params=pltpu.CompilerParams(vmem_limit_bytes=20 * 2**20),
        cost_estimate=pl.CostEstimate(
            flops=4 * own * count * embed,
            bytes_accessed=2 * count * embed + 6 * own * embed,
            transcendentals=own * count,
        ),
    )(at, params, made, others)


def body(img_feat, txt_feat, img_proj, txt_proj, logit_scale, logit_bias, loss_weight):
    bf16, f32 = jnp.bfloat16, jnp.float32
    scale, shift_by, weight = logit_scale[0], logit_bias[0], loss_weight[0]
    rows, width = img_feat.shape
    cols = img_proj.shape[1]
    blk = lax.axis_index("blk")
    grp = lax.axis_index("grp")
    core = grp % N_CORE
    x = (grp // N_CORE) % N_X
    zh = (grp // (N_CORE * N_X)) % N_ZH
    y = grp // (N_CORE * N_X * N_ZH)
    first = core == 0
    steps = jnp.where(zh == 0, blk, N_BLK - 1 - blk)
    sub = (steps & 1) * 4 + (steps & 2) + (steps & 4) // 4
    sub_rows = rows // N_BLK
    own = N_CORE * rows

    low = zh == 0
    img_t, txt_t = img_proj.T, txt_proj.T
    own_f, other_f = jnp.where(first, img_feat, txt_feat), jnp.where(first, txt_feat, img_feat)
    own_sub = lax.dynamic_slice_in_dim(own_f, sub * sub_rows, sub_rows, 0)
    other_sub = lax.dynamic_slice_in_dim(other_f, sub * sub_rows, sub_rows, 0)
    ours = jnp.concatenate([own_sub, jnp.where(first, img_t, txt_t)], 0)
    theirs = jnp.concatenate([other_sub, jnp.where(first, txt_t, img_t)], 0)

    def joined(mine, siblings):
        mine_t, siblings_t = mine[sub_rows:], siblings[sub_rows:]
        return jnp.concatenate(
            [
                mine[:sub_rows],
                siblings[:sub_rows],
                jnp.where(first, mine_t, siblings_t),
                jnp.where(first, siblings_t, mine_t),
            ],
            0,
        )

    far = joined(
        permuted(ours, mirror), permuted(theirs, lambda device: mirror(sibling(device)))
    )
    near = gathered(joined(ours, permuted(theirs, sibling)), INNER)
    far = gathered(far, INNER)
    picked = N_CORE * sub_rows
    pair = N_CORE * cols
    both = jnp.concatenate(
        [
            near[:, :picked],
            far[:, :picked],
            jnp.where(low, near[:, picked:], far[:, picked:]),
            jnp.where(low, far[:, picked:], near[:, picked:]),
        ],
        1,
    )
    sib_feat = permuted(jnp.concatenate([own_f, other_f], 0), sibling)
    sib_other, sib_own = sib_feat[:rows], sib_feat[rows:]

    def interleaved(one, two):
        shape = (N_BLK, sub_rows, width)
        return jnp.stack([one.reshape(shape), two.reshape(shape)], 1).reshape(own, width)

    feat = interleaved(other_f, sib_other)
    sib_rows = interleaved(sib_own, own_f)
    both, feat, sib_rows = lax.optimization_barrier((both, feat, sib_rows))

    both = gathered(both, OUTER)
    proj = both[:, :, N_ZH * picked :]
    flipped = proj.transpose(1, 0, 2, 3).reshape(-1, width)
    proj = proj.reshape(-1, width)
    embed = proj.shape[0]

    made = permuted(contract_last(sib_rows, flipped), sibling)
    others = both[:, :, : N_ZH * picked].reshape(N_Y * N_X, -1, width)
    others = embedded(others, N_ZH * picked, proj)
    spot = jnp.where(first, y * N_X + x, x * N_Y + y) * (N_ZH * picked)
    at = jnp.stack([sub * picked, spot]).astype(jnp.int32)
    part = partial_grads(at, jnp.stack([scale, shift_by, weight]), made, others, picked)

    terms = contract_first(part, feat).astype(bf16)
    part, terms, late_proj = lax.optimization_barrier((part, terms, flipped))
    terms = exchanged(terms.reshape(4, embed // 4, width), OUTER)
    terms = jnp.sum(terms.astype(f32), 0).astype(bf16)
    quarter = own // 4
    at_quarter = sub // 2

    def quarter_of(index):
        return lax.dynamic_slice_in_dim(part, index * quarter, quarter, 0)

    held = summed(
        quarter_of(at_quarter),
        permuted(quarter_of(at_quarter ^ 2), along(1)),
        permuted(quarter_of(at_quarter ^ 1), along(2)),
        permuted(quarter_of(at_quarter ^ 3), along(3)),
    ).astype(bf16)
    held, terms, late_proj = lax.optimization_barrier((held, terms, late_proj))
    terms = exchanged(terms.reshape(4, embed // 16, width), INNER)
    held = held.astype(f32) + permuted(held, along(4)).astype(f32)
    terms = jnp.sum(terms.astype(f32), 0)
    lower, upper = terms[:pair], terms[pair:]
    came = permuted(jnp.where(low, upper, lower).astype(bf16), mirror)
    du, came, other_proj = lax.optimization_barrier(
        (held.astype(bf16), came, permuted(late_proj, sibling))
    )
    pieces = [du] + [permuted(du, along(hop)) for hop in (2, 1, 3)]
    swap = (at_quarter & 1) == 1
    pieces = [jnp.where(swap, pieces[index ^ 1], pieces[index]) for index in range(4)]
    swap = (at_quarter & 2) == 2
    pieces = [jnp.where(swap, pieces[index ^ 2], pieces[index]) for index in range(4)]
    du = jnp.concatenate(pieces, 0)

    total = (jnp.where(low, lower, upper) + came.astype(f32)).astype(bf16)
    total = (total.astype(f32) + permuted(total, along(4)).astype(f32)).astype(bf16)
    total = summed(total, *(permuted(total, along(hop)) for hop in (1, 2, 3)))
    keep_g = jnp.where(first, total[:cols], total[cols:pair])
    got_g = permuted(jnp.where(first, total[cols:pair], total[:cols]), sibling)
    img_proj_grad = jnp.where(first, got_g, keep_g).T
    txt_proj_grad = jnp.where(first, keep_g, got_g).T

    grad = jnp.dot(du, other_proj, preferred_element_type=f32)
    grad = grad.reshape(N_BLK, N_CORE, sub_rows, width)
    keep_r = grad[:, 0].reshape(rows, width)
    got_r = permuted(grad[:, 1].reshape(rows, width), sibling)
    img_grad = jnp.where(first, got_r, keep_r)
    txt_grad = jnp.where(first, keep_r, got_r)
    return (img_grad, txt_grad, img_proj_grad, txt_proj_grad)


def solution(mesh):
    return jax.shard_map(
        body,
        mesh=mesh,
        in_specs=(P("grp", None), P("grp", None), P(None, "grp"), P(None, "grp"), P(), P(), P()),
        out_specs=(P("grp", None), P("grp", None), P(None, "grp"), P(None, "grp")),
        check_vma=False,
    )
```
